32 devices in a mesh: hist: 8 (over z, x), row: 4 (over y, core).
Axes of the slice: x: 2, y: 2, z: 4, core: 2. Of those that a mesh axis runs over, the one named last changes fastest.
Arguments:
- row_less: float32 [2, 96, 1024], P(None, 'hist'), may hold values from -40 to 40
- row_great: float32 [2, 96, 1024], P(None, 'hist'), may hold values from -5 to 5
- coupling: float32 [32, 32], replicated, may hold values from -1 to 1
- damping: float32 [96, 32], P('hist'), may hold values from 0.2 to 1, as said below
- phases: float32 [96, 32], P('hist'), may hold values from -3.140625 to 3.140625
- lesser_hist: bfloat16 [2, 96, 96, 1024], P(None, 'row', 'hist'), may hold values from -5 to 5
- advanced_hist: bfloat16 [2, 96, 96, 1024], P(None, 'row', 'hist'), may hold values from -5 to 5
- retarded_hist: bfloat16 [2, 96, 96, 1024], P(None, 'row', 'hist'), may hold values from -5 to 5
Outputs:
- stepped_row: float32 [2, 96, 1024], P(None, 'hist')
- column_term: float32 [2, 96, 1024], P(None, 'row')
The draws below stay inside these ranges and needn't reach their ends.
Inputs may be any that keep to these rules, and one draw needn't show every extreme that they name: `damping`: one-step magnitudes.
All inputs are finite; a program needn't handle non-finite values.
Results may differ from the reference program's by a relative error of at most 0.0029.
Values may be sent and summed in bfloat16 or wider, within the bound.
No kernel may reach another device: no remote copies, remote signals or barrier semaphores. Data moves between devices by JAX's collectives and lax.ppermute only.
A program may use at most 128 MiB of HBM per device.

```python
import math
import jax
import jax.numpy as jnp
from jax import lax

NB = 32
TP = 12
PAST_TIME_SLICES = 96
N_HIST = 8


def draw_row_less(key, part):
    key = jax.random.fold_in(key, 5)
    key_cols, key_base = jax.random.split(key, 2)
    col_scale = jnp.exp(jax.random.uniform(key_cols, (NB * NB,), jnp.float32, math.log(0.4), math.log(4.0)))
    base = jnp.clip(jax.random.normal(key_base, (2, PAST_TIME_SLICES, NB * NB), jnp.float32), -3.5, 3.5)
    values = base * col_scale[None, None, :]
    return values.astype(jnp.float32)


def draw_damping(key, part):
    key = jax.random.fold_in(key, 11)
    key_fast, key_len, key_rough, random_seed_slot, key_depth = jax.random.split(key, 5)
    fast_percent = 50
    fast = jax.random.randint(key_fast, (NB,), 0, 100) < fast_percent
    fast_len = jax.random.uniform(key_len, (NB,), jnp.float32, 15.0, 25.0)
    slow_len = jax.random.uniform(key_len, (NB,), jnp.float32, 3.0 * PAST_TIME_SLICES, 5.0 * PAST_TIME_SLICES)
    length = jnp.where(fast, fast_len, slow_len)
    rough = jax.random.uniform(key_rough, (PAST_TIME_SLICES, NB), jnp.float32, 0.5, 2.0)
    attenuation_speed = jnp.exp(-rough / length[None, :])
    spike_instant = jax.random.randint(random_seed_slot, (3,), 0, PAST_TIME_SLICES)
    memory_length = jax.random.uniform(key_depth, (3, NB), jnp.float32, 0.65, 0.85)
    spike_arrival = jnp.arange(PAST_TIME_SLICES, dtype=jnp.int32)[:, None] == spike_instant[None, :]
    spike_occurrence = jnp.prod(jnp.where(spike_arrival[:, :, None], memory_length[None, :, :], 1.0), axis=1)
    return (attenuation_speed * spike_occurrence).astype(jnp.float32)


def shard_levels(key, shape, cuts, low, top_value):
    factor_of, own = 1.0, jax.random.fold_in(key, 6)
    for axis_at, blocks in cuts:
        heights = jnp.exp(jax.random.uniform(jax.random.fold_in(own, axis_at), (blocks,), jnp.float32, low / len(cuts), top_value / len(cuts)))
        factor_of = factor_of * jnp.repeat(heights, shape[axis_at] // blocks).reshape([-1 if axis == axis_at else 1 for axis in range(len(shape))])
    return factor_of


def noise(stream_key, dims, deviation, limit, shards=(), held_as=jnp.bfloat16):
    result = deviation * jax.random.normal(stream_key, dims, jnp.float32)
    if shards:
        result = result * shard_levels(stream_key, dims, shards, -0.22, 0.18)
    return jnp.clip(result, -limit, limit).astype(held_as)


def setup_inputs(seed: int = 0) -> dict:
    key_of = jax.random.split(jax.random.key(seed), 9)
    row_less = draw_row_less(jax.random.fold_in(key_of[8], 71), 0)
    row_great = noise(key_of[1], (2, PAST_TIME_SLICES, NB * NB), 1.0, 5.0, ((1, 8),), jnp.float32)
    coupling = noise(key_of[2], (NB, NB), NB ** -0.5, 1.0, (), jnp.float32)
    damping = draw_damping(jax.random.fold_in(key_of[8], 71), 0)
    phases = jnp.clip(jax.random.uniform(key_of[4], (PAST_TIME_SLICES, NB), jnp.float32, -3.140625, 3.140625), -3.140625, 3.140625)
    lesser_hist = noise(key_of[5], (2, PAST_TIME_SLICES, PAST_TIME_SLICES, NB * NB), 1.0, 5.0, ((1, 4), (2, 8)))
    advanced_hist = noise(key_of[6], (2, PAST_TIME_SLICES, PAST_TIME_SLICES, NB * NB), 1.0, 5.0, ((1, 4), (2, 8)))
    retarded_hist = noise(key_of[7], (2, PAST_TIME_SLICES, PAST_TIME_SLICES, NB * NB), 1.0, 5.0, ((1, 4), (2, 8)))
    return {"row_less": row_less, "row_great": row_great, "coupling": coupling, "damping": damping, "phases": phases, "lesser_hist": lesser_hist, "advanced_hist": advanced_hist, "retarded_hist": retarded_hist}


def self_energy(row_less, row_great, coupling):
    steps_here = row_less.shape[1]
    bands = coupling.shape[0]
    less_real = row_less[0].reshape(steps_here, bands, bands)
    less_imag = row_less[1].reshape(steps_here, bands, bands)
    great_real = row_great[0].reshape(steps_here, bands, bands)
    great_imag = row_great[1].reshape(steps_here, bands, bands)
    polar_real = -(less_real * great_real + less_imag * great_imag)
    polar_imag = -(less_imag * great_real - less_real * great_imag)
    highest = lax.Precision.HIGHEST

    def sandwich(polar):
        partial_value = jnp.einsum('ik,skl->sil', coupling, polar, precision=highest)
        return jnp.einsum('sil,jl->sij', partial_value, coupling, precision=highest)
    screen_real = sandwich(polar_real)
    screen_imag = sandwich(polar_imag)
    sigma_less = jnp.stack([less_real * screen_real - less_imag * screen_imag, less_real * screen_imag + less_imag * screen_real])
    sigma_great = jnp.stack([great_real * screen_real + great_imag * screen_imag, great_imag * screen_real - great_real * screen_imag])
    return ((sigma_great - sigma_less).astype(jnp.bfloat16), sigma_less.astype(jnp.bfloat16))

def reference(row_less, row_great, coupling, damping, phases, lesser_hist, advanced_hist, retarded_hist):
    weight = float(PAST_TIME_SLICES * NB) ** (-0.5)
    sigma_ret, sigma_less = self_energy(row_less, row_great, coupling)
    ret_wide = sigma_ret.astype(jnp.float32)
    less_wide = sigma_less.astype(jnp.float32)
    positions = jnp.arange(PAST_TIME_SLICES, dtype=jnp.int32)

    def contract_row(sigma, hist):
        return jnp.einsum('sik,stkj->tij', sigma, hist)

    def row_block(block_index):
        offset = (block_index * TP).astype(jnp.int32)
        lesser = lax.dynamic_slice_in_dim(lesser_hist, offset, TP, 2).astype(jnp.float32).reshape(2, PAST_TIME_SLICES, TP, NB, NB)
        advanced = lax.dynamic_slice_in_dim(advanced_hist, offset, TP, 2).astype(jnp.float32).reshape(2, PAST_TIME_SLICES, TP, NB, NB)
        target_steps = offset + jnp.arange(TP, dtype=jnp.int32)
        causal = positions[:, None] <= target_steps[None, :]
        advanced = jnp.where(causal[None, :, :, None, None], advanced, jnp.zeros((), jnp.float32))
        real_part = contract_row(ret_wide[0], lesser[0]) - contract_row(ret_wide[1], lesser[1]) + contract_row(less_wide[0], advanced[0]) - contract_row(less_wide[1], advanced[1])
        imag_part = contract_row(ret_wide[0], lesser[1]) + contract_row(ret_wide[1], lesser[0]) + contract_row(less_wide[0], advanced[1]) + contract_row(less_wide[1], advanced[0])
        return weight * jnp.stack([real_part, imag_part])
    blocks = lax.map(row_block, jnp.arange(N_HIST, dtype=jnp.int32))
    collision = blocks.transpose(1, 0, 2, 3, 4).reshape(2, PAST_TIME_SLICES, NB * NB)

    def contract_column(hist, sigma):
        return jnp.einsum('tsik,sjk->tij', hist, sigma)

    def column_block(block_index):
        offset = (block_index * TP).astype(jnp.int32)
        retarded = lax.dynamic_slice_in_dim(retarded_hist, offset, TP, 1).astype(jnp.float32).reshape(2, TP, PAST_TIME_SLICES, NB, NB)
        later_steps = offset + jnp.arange(TP, dtype=jnp.int32)
        causal = positions[None, :] <= later_steps[:, None]
        retarded = jnp.where(causal[None, :, :, None, None], retarded, jnp.zeros((), jnp.float32))
        real_part = -(contract_column(retarded[0], less_wide[0]) + contract_column(retarded[1], less_wide[1]))
        imag_part = -(contract_column(retarded[1], less_wide[0]) - contract_column(retarded[0], less_wide[1]))
        return weight * jnp.stack([real_part, imag_part])
    column_blocks = lax.map(column_block, jnp.arange(N_HIST, dtype=jnp.int32))
    column_term = column_blocks.transpose(1, 0, 2, 3, 4).reshape(2, PAST_TIME_SLICES, NB * NB)
    log_rate = jnp.log(damping)
    summed_log = jnp.cumsum(log_rate[::-1], axis=0)[::-1]
    summed_phase = jnp.cumsum(phases[::-1], axis=0)[::-1]
    magnitude = jnp.exp(summed_log)
    factor_real = jnp.repeat(magnitude * jnp.cos(summed_phase), NB, axis=1)
    factor_imag = jnp.repeat(-magnitude * jnp.sin(summed_phase), NB, axis=1)
    sum_real = row_less[0] + collision[0]
    sum_imag = row_less[1] + collision[1]
    stepped_real = factor_real * sum_real - factor_imag * sum_imag
    stepped_imag = factor_real * sum_imag + factor_imag * sum_real
    squares = jnp.sum(stepped_real * stepped_real) + jnp.sum(stepped_imag * stepped_imag)
    norm_scale = jnp.sqrt(squares / (2 * PAST_TIME_SLICES * NB * NB) + 1e-06)
    stepped_row = jnp.stack([stepped_real, stepped_imag]) / norm_scale
    return (stepped_row, column_term)
```

```python
import functools

import jax
import jax.numpy as jnp
from jax import lax
from jax.experimental import pallas as pl
from jax.experimental.pallas import tpu as pltpu
from jax.sharding import PartitionSpec as P

F32, BF16 = (jnp.float32, jnp.bfloat16)
HIGHEST = lax.Precision.HIGHEST
EXTRA = 16
VMEM_LIMIT = 48 * 1024 * 1024


def swap_places(x, turn):
    hist_count, row_count = (lax.axis_size("hist"), lax.axis_size("row"))
    ratio = hist_count // row_count
    cores = 2 if row_count % 2 == 0 else 1
    span = row_count // cores
    pairs = []
    for slow in range(row_count):
        for fast in range(ratio):
            for row in range(row_count):
                source = (slow * ratio + fast) * row_count + row
                goal = row % cores * span + (row // cores + 1 + turn) % span
                target = (goal * ratio + (fast + turn) % ratio) * row_count + slow
                pairs.append((source, target))
    return lax.ppermute(x, ("hist", "row"), pairs)


def crossed(x, axis, bit):
    size = lax.axis_size(axis)
    return lax.ppermute(x, axis, [(k, k ^ bit) for k in range(size)])


def lane_block(shape, width):
    return lax.broadcasted_iota(jnp.int32, shape, len(shape) - 1) // width


def swap_blocks(parts):
    width = parts[0].shape[1] // 4
    block = lane_block(parts[0].shape, width)
    parts = list(parts)
    for bit in (2, 1):
        new = list(parts)
        for a in range(4):
            if a & bit == 0:
                low, high = (parts[a], parts[a | bit])
                shift = bit * width
                keep = block & bit == 0
                new[a] = jnp.where(keep, low, pltpu.roll(high, shift, 1))
                new[a | bit] = jnp.where(keep, pltpu.roll(low, 4 * width - shift, 1), high)
        parts = new
    return parts


def energy_kernel(bands, steps, order_ref, less_ref, great_ref, coupling_ref, damping_ref, phases_ref, send_ref, packed_ref, work):
    groups = bands // 4
    chunks = steps // 4
    for which, ref in enumerate((less_ref, great_ref)):
        for part in range(2):
            for chunk in range(chunks):
                blocks = [
                    ref[pl.ds((chunk * 4 + k) * groups * 2 + part, groups, stride=2), :]
                    for k in range(4)
                ]
                for k, block in enumerate(swap_blocks(blocks)):
                    work[which, part, pl.ds(chunk * bands + k, groups, stride=4), :] = block
    less_real, less_imag = (work[0, 0], work[0, 1])
    great_real, great_imag = (work[1, 0], work[1, 1])
    polar = jnp.concatenate(
        [
            -(less_real * great_real + less_imag * great_imag),
            -(less_imag * great_real - less_real * great_imag),
        ],
        axis=0,
    )
    coupling = coupling_ref[...]
    wide = jnp.concatenate([coupling] * 4, axis=1)
    tall = jnp.concatenate([wide] * 4, axis=0)
    at_row = lax.broadcasted_iota(jnp.int32, tall.shape, 0) // bands
    blocked = jnp.where(at_row == lane_block(tall.shape, bands), tall, 0.0)
    half = lax.dot_general(
        polar, blocked, (((1,), (1,)), ((), ())), precision=HIGHEST, preferred_element_type=F32
    )
    rows = chunks * bands
    both = jnp.concatenate([half[:rows], half[rows:]], axis=1)
    screens = []
    for chunk in range(chunks):
        screens.append(
            jnp.dot(
                coupling,
                both[chunk * bands : (chunk + 1) * bands],
                precision=HIGHEST,
                preferred_element_type=F32,
            )
        )
    screen = jnp.concatenate(screens, axis=0)
    lanes = 4 * bands
    screen_real, screen_imag = (screen[:, :lanes], screen[:, lanes:])
    sigma_real = less_real * screen_real - less_imag * screen_imag
    sigma_imag = less_real * screen_imag + less_imag * screen_real
    wide_real = great_real * screen_real + great_imag * screen_imag
    wide_imag = great_imag * screen_real - great_real * screen_imag
    outs = (wide_real - sigma_real, wide_imag - sigma_imag, sigma_real, sigma_imag)
    for chunk in range(chunks):
        at = slice(chunk * bands, (chunk + 1) * bands)
        to = slice(chunk * lanes, (chunk + 1) * lanes)
        for k, out in enumerate(outs):
            first = (chunk * 4 + k) * bands
            send_ref[first : first + bands, :] = out[at].astype(BF16)
        packed_ref[:bands, to] = less_real[at]
        packed_ref[bands:, to] = less_imag[at]
    log_total = jnp.sum(jnp.log(damping_ref[...]), axis=0, keepdims=True)
    phase_total = jnp.sum(phases_ref[...], axis=0, keepdims=True)
    last = steps * bands
    send_ref[last:, :] = jnp.zeros((EXTRA, lanes), BF16)
    send_ref[last:, :bands] = pieces_of((log_total, phase_total)).astype(BF16)


def order_kernel(bands, steps, ratio, order_ref):
    groups = bands // 4
    padded = order_ref.shape[1] // bands
    taken = steps * bands
    source = lax.broadcasted_iota(jnp.int32, (taken, 1), 0)
    band = source % bands
    target = (band % 4) * (groups * padded) + (band // 4) * padded + source // bands
    column = lax.broadcasted_iota(jnp.int32, (taken, order_ref.shape[1]), 1)
    for turn in range(ratio):
        fast = (lax.axis_index("hist") + ratio - turn) % ratio
        hit = column == target + fast * steps
        order_ref[turn * taken : (turn + 1) * taken, :] = jnp.where(hit, 1.0, 0.0).astype(BF16)


def column_kernel(bands, steps, rows, weight, retarded_ref, send_ref, keep_ref, give_ref):
    lanes = 4 * bands
    groups = bands // 4
    hist_start, row_start = (lax.axis_index("hist") * steps, lax.axis_index("row") * rows)
    block = lane_block((bands, lanes), bands)
    later = row_start + lax.broadcasted_iota(jnp.int32, (rows, groups * lanes), 0)
    total = None
    for chunk in range(steps // 4):
        turned = []
        for part in range(2):
            first = (chunk * 4 + 2 + part) * bands
            own = send_ref[first : first + bands, :].astype(F32)
            turned.append([own] + [pltpu.roll(own, d * bands, 1) for d in range(1, 4)])
        for k in range(4):
            step = chunk * 4 + k
            real, imag = [
                jnp.concatenate(
                    [jnp.where(block == b, turned[part][(b - k) % 4], 0.0) for b in range(4)],
                    axis=0,
                )
                for part in range(2)
            ]
            weights = jnp.concatenate(
                [
                    jnp.concatenate([real, imag], axis=1),
                    jnp.concatenate([-imag, real], axis=1),
                ],
                axis=0,
            ).astype(BF16)
            causal = hist_start + step <= later
            halves = []
            for part in range(2):
                whole = jnp.where(causal, retarded_ref[part, step].astype(F32), 0.0)
                halves.append(
                    jnp.concatenate(
                        [whole[:, g * lanes : (g + 1) * lanes] for g in range(groups)], axis=0
                    ).astype(BF16)
                )
            term = lax.dot_general(
                jnp.concatenate(halves, axis=1),
                weights,
                (((1,), (1,)), ((), ())),
                preferred_element_type=F32,
            )
            total = term if total is None else total + term
    low = lax.axis_index("hist") % 2 == 0
    for g in range(groups // 2):
        for part in range(2):
            halves = [
                -weight * total[k * rows : (k + 1) * rows, part * lanes : (part + 1) * lanes]
                for k in (g, g + groups // 2)
            ]
            to = slice((2 * g + part) * rows, (2 * g + part + 1) * rows)
            keep_ref[to, :] = jnp.where(low, halves[0], halves[1])
            give_ref[to, :] = jnp.where(low, halves[1], halves[0])


def add_kernel(own_ref, other_ref, out_ref):
    total = own_ref[...].astype(F32) + other_ref[...].astype(F32)
    out_ref[...] = total.astype(out_ref.dtype)


def final_kernel(count, stepped_ref, own_ref, other_ref, sum_ref, more_ref, row_ref, column_ref):
    squares = (own_ref[...] + other_ref[...])[0:1]
    row_ref[...] = stepped_ref[...] / jnp.sqrt(squares / count + 1e-06)
    low = lax.axis_index("hist") % 2 == 0
    half, back = (sum_ref[...], more_ref[...])
    column = jnp.concatenate([jnp.where(low, half, back), jnp.where(low, back, half)], axis=0)
    rows, lanes = (column_ref.shape[1], column.shape[1])
    for part in range(2):
        for g in range(column_ref.shape[2] // lanes):
            at = (2 * g + part) * rows
            column_ref[part, :, g * lanes : (g + 1) * lanes] = column[at : at + rows]


def row_kernel(bands, steps, rows, weight, ratio, order_ref, lesser_ref, advanced_ref, *refs):
    arrived_refs, out_ref = (refs[:ratio], refs[ratio])
    lanes = 4 * bands
    groups = bands // 4
    padded = order_ref.shape[1] // bands
    depth = groups * padded
    taken = steps * bands
    ordered = None
    for turn, ref in enumerate(arrived_refs):
        sigma = jnp.concatenate([ref[c * lanes : (c + 1) * lanes, :] for c in range(steps // 4)], axis=1)
        term = jnp.dot(
            sigma,
            order_ref[turn * taken : (turn + 1) * taken, :],
            preferred_element_type=F32,
        )
        ordered = term if ordered is None else ordered + term
    lefts = []
    for which in range(2):
        real = ordered[2 * which * bands : (2 * which + 1) * bands]
        imag = ordered[(2 * which + 1) * bands : (2 * which + 2) * bands]
        for pair in ((real, imag), (-imag, real)):
            lefts.append(
                jnp.concatenate(
                    [part[:, k * depth : (k + 1) * depth] for k in range(4) for part in pair],
                    axis=0,
                ).astype(BF16)
            )
    hist_start, row_start = (lax.axis_index("hist") * steps, lax.axis_index("row") * rows)
    earlier = row_start + lax.broadcasted_iota(jnp.int32, (rows, groups * lanes), 0)
    filler = jnp.zeros((padded - rows, lanes), F32)

    def right(which, part, step):
        ref = (lesser_ref, advanced_ref)[which]
        whole = ref[part, step].astype(F32)
        if which == 1:
            whole = jnp.where(earlier <= hist_start + step, whole, 0.0)
        pieces = []
        for g in range(groups):
            pieces.append(whole[:, g * lanes : (g + 1) * lanes])
            if padded > rows:
                pieces.append(filler)
        return jnp.concatenate(pieces, axis=0).astype(BF16)

    block = lane_block((2 * bands, lanes), bands)
    for chunk in range(steps // 4):
        gathered = None
        for pair in range(2):
            first = chunk * 4 + pair * 2
            total = None
            for which in range(2):
                for part in range(2):
                    rights = jnp.concatenate(
                        [right(which, part, first), right(which, part, first + 1)], axis=1
                    )
                    term = jnp.dot(
                        lefts[2 * which + part], rights, preferred_element_type=F32
                    )
                    total = term if total is None else total + term
            for k in range(2):
                own = total[:, k * lanes : (k + 1) * lanes]
                picked = own[: 2 * bands]
                for b in range(1, 4):
                    picked = jnp.where(block == b, own[2 * bands * b : 2 * bands * (b + 1)], picked)
                picked = picked + pltpu.roll(picked, 2 * bands, 1)
                picked = picked + pltpu.roll(picked, bands, 1)
                gathered = (
                    picked if gathered is None else jnp.where(block == 2 * pair + k, picked, gathered)
                )
        out_ref[: 2 * bands, chunk * lanes : (chunk + 1) * lanes] = weight * gathered
    above_log = jnp.zeros((1, bands), F32)
    above_phase = jnp.zeros((1, bands), F32)
    for turn, ref in enumerate(arrived_refs):
        fast = (lax.axis_index("hist") + ratio - turn) % ratio
        later = jnp.where(lax.axis_index("row") * ratio + fast > lax.axis_index("hist"), 1.0, 0.0)
        extra = ref[taken:, :bands].astype(F32)
        above_log = above_log + later * (extra[0:1] + extra[1:2] + extra[2:3])
        above_phase = above_phase + later * (extra[3:4] + extra[4:5] + extra[5:6])
    at = lax.broadcasted_iota(jnp.int32, (8, bands), 0)
    out_ref[2 * bands :, :] = jnp.zeros((8, steps * bands), F32)
    out_ref[2 * bands :, :bands] = jnp.where(at == 0, above_log, jnp.where(at == 1, above_phase, 0.0))


def pieces_of(totals):
    shape = (EXTRA, totals[0].shape[1])
    row = lax.broadcasted_iota(jnp.int32, shape, 0)
    extra = jnp.zeros(shape, F32)
    at = 0
    for total in totals:
        for _ in range(3):
            piece = total.astype(BF16).astype(F32)
            extra = jnp.where(row == at, piece, extra)
            total = total - piece
            at += 1
    return extra


def narrow_kernel(bands, own_ref, other_ref, out_ref):
    total = own_ref[...] + other_ref[...]
    lanes = 4 * bands
    last = total.shape[1] // lanes * 2 * bands
    for k in range(total.shape[1] // lanes):
        part = total[: 2 * bands, k * lanes : (k + 1) * lanes]
        out_ref[2 * bands * k : 2 * bands * (k + 1), :] = part.astype(BF16)
    out_ref[last:, :] = jnp.zeros((EXTRA, lanes), BF16)
    above = total[2 * bands :, :bands]
    out_ref[last:, :bands] = pieces_of((above[0:1], above[1:2])).astype(BF16)


def step_kernel(
    bands, steps, damping_ref, phases_ref, packed_ref, own_ref, other_ref,
    out_ref, square_ref, work
):
    lanes = 4 * bands
    groups = bands // 4
    last = steps // 4 * 2 * bands
    extra = own_ref[last:, :bands].astype(F32) + other_ref[last:, :bands].astype(F32)
    above_log = extra[0:1] + extra[1:2] + extra[2:3]
    above_phase = extra[3:4] + extra[4:5] + extra[5:6]
    at = lax.broadcasted_iota(jnp.int32, (steps, bands), 0)
    rates = jnp.log(damping_ref[...])
    phases = phases_ref[...]
    summed_log = jnp.broadcast_to(above_log, (steps, bands))
    summed_phase = jnp.broadcast_to(above_phase, (steps, bands))
    for step in range(steps):
        summed_log = summed_log + jnp.where(at <= step, rates[step : step + 1], 0.0)
        summed_phase = summed_phase + jnp.where(at <= step, phases[step : step + 1], 0.0)
    magnitude = jnp.exp(summed_log)
    both = jnp.concatenate(
        [magnitude * jnp.cos(summed_phase), -magnitude * jnp.sin(summed_phase)], axis=1
    )
    wide = lax.broadcasted_iota(jnp.int32, (steps, steps * bands), 1) // bands
    place = lax.broadcasted_iota(jnp.int32, (steps, steps * bands), 0)
    spreading = jnp.where(wide == place, 1.0, 0.0)
    factor = lax.dot_general(
        both, spreading, (((0,), (0,)), ((), ())), precision=HIGHEST, preferred_element_type=F32
    )
    collision = own_ref[:last, :].astype(F32) + other_ref[:last, :].astype(F32)
    chunks = [collision[2 * bands * k : 2 * bands * (k + 1)] for k in range(steps // 4)]
    row = packed_ref[...] + jnp.concatenate(chunks, axis=1)
    row_real, row_imag = (row[:bands], row[bands:])
    factor_real, factor_imag = (factor[:bands], factor[bands:])
    stepped = (
        factor_real * row_real - factor_imag * row_imag,
        factor_real * row_imag + factor_imag * row_real,
    )
    squares = jnp.sum(stepped[0] * stepped[0] + stepped[1] * stepped[1], keepdims=True)
    square_ref[...] = jnp.broadcast_to(squares, square_ref.shape)
    for part in range(2):
        for chunk in range(steps // 4):
            work[part, chunk] = stepped[part][:, chunk * lanes : (chunk + 1) * lanes]
    for part in range(2):
        for chunk in range(steps // 4):
            blocks = [work[part, chunk, pl.ds(k, groups, stride=4), :] for k in range(4)]
            for k, block in enumerate(swap_blocks(blocks)):
                first = (chunk * 4 + k) * groups * 2 + part
                out_ref[pl.ds(first, groups, stride=2), :] = block


def call(kernel, shapes, scratch, flops, moved, spaces, *operands):
    return pl.pallas_call(
        kernel,
        out_shape=shapes,
        in_specs=[pl.BlockSpec(memory_space=space) for space in spaces],
        out_specs=[pl.BlockSpec(memory_space=pltpu.VMEM)] * len(shapes),
        scratch_shapes=scratch,
        compiler_params=pltpu.CompilerParams(vmem_limit_bytes=VMEM_LIMIT),
        cost_estimate=pl.CostEstimate(flops=flops, bytes_accessed=moved, transcendentals=0),
    )(*operands)


def shards(
    row_less, row_great, coupling, damping, phases, lesser_hist, advanced_hist, retarded_hist
):
    bands = coupling.shape[0]
    lanes = 4 * bands
    groups = bands // 4
    steps = row_less.shape[1]
    rows = lesser_hist.shape[1]
    hist_count, row_count = (lax.axis_size("hist"), lax.axis_size("row"))
    ratio = hist_count // row_count
    all_steps = steps * hist_count
    weight = float(all_steps * bands) ** (-0.5)
    padded = -(-rows // 16) * 16
    taken = steps * bands
    sds = jax.ShapeDtypeStruct

    def grouped(x):
        x = x.reshape(2, steps, groups, lanes).transpose(1, 2, 0, 3)
        return x.reshape(steps * groups * 2, lanes)

    retarded = retarded_hist.transpose(0, 2, 1, 3)
    vmem = pltpu.VMEM
    (order,) = call(
        functools.partial(order_kernel, bands, steps, ratio),
        [sds((ratio * taken, bands * padded), BF16)],
        [],
        10**10,
        10**7,
        [],
    )
    send, packed = call(
        functools.partial(energy_kernel, bands, steps),
        [sds((taken + EXTRA, lanes), BF16), sds((2 * bands, taken), F32)],
        [vmem((2, 2, steps // 4 * bands, lanes), F32)],
        10**8,
        10**6,
        [pl.ANY] + [vmem] * 5,
        order,
        grouped(row_less),
        grouped(row_great),
        coupling,
        damping,
        phases,
    )
    arrived = [swap_places(send, turn) for turn in range(ratio)]
    column, give = call(
        functools.partial(column_kernel, bands, steps, rows, weight),
        [sds((groups * rows, lanes), F32)] * 2,
        [],
        10**9,
        4 * 10**6,
        [vmem] * 2,
        retarded,
        send,
    )

    def add(own, other, kind):
        (out,) = call(
            add_kernel, [sds(own.shape, kind)], [], 10**10, 10**6, [vmem] * 2, own, other
        )
        return out

    got = crossed(give, "hist", 1)
    order, got = lax.optimization_barrier((order, got))
    (partial_row,) = call(
        functools.partial(row_kernel, bands, steps, rows, weight, ratio),
        [sds((2 * bands + 8, taken), F32)],
        [],
        10**6,
        10**6,
        [vmem] * (3 + ratio),
        order,
        lesser_hist.transpose(0, 2, 1, 3),
        advanced_hist.transpose(0, 2, 1, 3),
        *arrived,
    )
    other = crossed(partial_row, "row", 1)
    bit = 2
    while 2 * bit < row_count:
        partial_row = add(partial_row, other, F32)
        other = crossed(partial_row, "row", bit)
        bit *= 2
    (narrow,) = call(
        functools.partial(narrow_kernel, bands),
        [sds((steps // 4 * 2 * bands + EXTRA, lanes), BF16)],
        [],
        10**6,
        10**6,
        [vmem] * 2,
        partial_row,
        other,
    )
    other = crossed(narrow, "row", bit)
    column = add(column, got, BF16)
    got = crossed(column, "hist", hist_count // 2)
    stepped, squares = call(
        functools.partial(step_kernel, bands, steps),
        [sds((steps * groups * 2, lanes), F32), sds((8, lanes), F32)],
        [vmem((2, steps // 4, bands, lanes), F32)],
        10**10,
        10**6,
        [vmem] * 5,
        damping,
        phases,
        packed,
        narrow,
        other,
    )
    ahead = [hist_count >> k for k in range(1, hist_count.bit_length() - 1)]
    beside = ahead[1:] + [1, None]
    for bit, each in zip([1] + ahead, beside):
        other = crossed(squares, "hist", bit)
        if each:
            column = add(column, got, BF16 if each == 2 else F32)
            got = crossed(column, "hist", each)
            squares = add(squares, other, F32)
    got, other = lax.optimization_barrier((got, other))
    stepped, column = call(
        functools.partial(final_kernel, float(2 * all_steps * bands * bands)),
        [sds(stepped.shape, F32), sds((2, rows, bands * bands), F32)],
        [],
        10**6,
        10**6,
        [vmem] * 5,
        stepped,
        squares,
        other,
        column,
        got,
    )
    stepped = stepped.reshape(steps, groups, 2, lanes).transpose(2, 0, 1, 3)
    return (stepped.reshape(2, steps, bands * bands), column)


def solution(mesh):
    return jax.shard_map(
        shards,
        mesh=mesh,
        in_specs=(
            P(None, "hist", None),
            P(None, "hist", None),
            P(),
            P("hist", None),
            P("hist", None),
            P(None, "row", "hist", None),
            P(None, "row", "hist", None),
            P(None, "row", "hist", None),
        ),
        out_specs=(P(None, "hist", None), P(None, "row", None)),
        check_vma=False,
    )
```

```python
import functools

import jax
import jax.numpy as jnp
from jax import lax
from jax.experimental import pallas as pl
from jax.experimental.pallas import tpu as pltpu
from jax.sharding import PartitionSpec as P

F32, BF16 = (jnp.float32, jnp.bfloat16)
HIGHEST = lax.Precision.HIGHEST
EXTRA = 16
WINDOW = 16
VMEM_LIMIT = 48 * 1024 * 1024


def swap_places(x, turn):
    hist_count, row_count = (lax.axis_size("hist"), lax.axis_size("row"))
    ratio = hist_count // row_count
    cores = 2 if row_count % 2 == 0 else 1
    span = row_count // cores
    pairs = []
    for slow in range(row_count):
        for fast in range(ratio):
            for row in range(row_count):
                source = (slow * ratio + fast) * row_count + row
                goal = row % cores * span + (row // cores + 1 + turn) % span
                target = (goal * ratio + (fast + turn) % ratio) * row_count + slow
                pairs.append((source, target))
    return lax.ppermute(x, ("hist", "row"), pairs)


def crossed(x, axis, bit):
    size = lax.axis_size(axis)
    return lax.ppermute(x, axis, [(k, k ^ bit) for k in range(size)])


def lane_block(shape, width):
    return lax.broadcasted_iota(jnp.int32, shape, len(shape) - 1) // width


def swap_blocks(parts):
    width = parts[0].shape[1] // 4
    block = lane_block(parts[0].shape, width)
    parts = list(parts)
    for bit in (2, 1):
        new = list(parts)
        for a in range(4):
            if a & bit == 0:
                low, high = (parts[a], parts[a | bit])
                shift = bit * width
                keep = block & bit == 0
                new[a] = jnp.where(keep, low, pltpu.roll(high, shift, 1))
                new[a | bit] = jnp.where(keep, pltpu.roll(low, 4 * width - shift, 1), high)
        parts = new
    return parts


def energy_kernel(bands, steps, order_ref, less_ref, great_ref, coupling_ref, damping_ref, phases_ref, send_ref, packed_ref, work):
    groups = bands // 4
    chunks = steps // 4
    for which, ref in enumerate((less_ref, great_ref)):
        for part in range(2):
            for chunk in range(chunks):
                blocks = [
                    ref[pl.ds((chunk * 4 + k) * groups * 2 + part, groups, stride=2), :]
                    for k in range(4)
                ]
                for k, block in enumerate(swap_blocks(blocks)):
                    work[which, part, pl.ds(chunk * bands + k, groups, stride=4), :] = block
    less_real, less_imag = (work[0, 0], work[0, 1])
    great_real, great_imag = (work[1, 0], work[1, 1])
    polar = jnp.concatenate(
        [
            -(less_real * great_real + less_imag * great_imag),
            -(less_imag * great_real - less_real * great_imag),
        ],
        axis=0,
    )
    coupling = coupling_ref[...]
    wide = jnp.concatenate([coupling] * 4, axis=1)
    tall = jnp.concatenate([wide] * 4, axis=0)
    at_row = lax.broadcasted_iota(jnp.int32, tall.shape, 0) // bands
    blocked = jnp.where(at_row == lane_block(tall.shape, bands), tall, 0.0)
    half = lax.dot_general(
        polar, blocked, (((1,), (1,)), ((), ())), precision=HIGHEST, preferred_element_type=F32
    )
    rows = chunks * bands
    both = jnp.concatenate([half[:rows], half[rows:]], axis=1)
    screens = []
    for chunk in range(chunks):
        screens.append(
            jnp.dot(
                coupling,
                both[chunk * bands : (chunk + 1) * bands],
                precision=HIGHEST,
                preferred_element_type=F32,
            )
        )
    screen = jnp.concatenate(screens, axis=0)
    lanes = 4 * bands
    screen_real, screen_imag = (screen[:, :lanes], screen[:, lanes:])
    sigma_real = less_real * screen_real - less_imag * screen_imag
    sigma_imag = less_real * screen_imag + less_imag * screen_real
    wide_real = great_real * screen_real + great_imag * screen_imag
    wide_imag = great_imag * screen_real - great_real * screen_imag
    outs = (wide_real - sigma_real, wide_imag - sigma_imag, sigma_real, sigma_imag)
    for chunk in range(chunks):
        at = slice(chunk * bands, (chunk + 1) * bands)
        to = slice(chunk * lanes, (chunk + 1) * lanes)
        for k, out in enumerate(outs):
            first = (chunk * 4 + k) * bands
            send_ref[first : first + bands, :] = out[at].astype(BF16)
        packed_ref[:bands, to] = less_real[at]
        packed_ref[bands:, to] = less_imag[at]
    log_total = jnp.sum(jnp.log(damping_ref[...]), axis=0, keepdims=True)
    phase_total = jnp.sum(phases_ref[...], axis=0, keepdims=True)
    last = steps * bands
    send_ref[last:, :] = jnp.zeros((EXTRA, lanes), BF16)
    send_ref[last:, :bands] = pieces_of((log_total, phase_total)).astype(BF16)


def order_kernel(bands, steps, ratio, order_ref):
    groups = bands // 4
    taken = steps * bands
    source = lax.broadcasted_iota(jnp.int32, (taken, 1), 0)
    band = source % bands
    target = (band % 4) * (groups * WINDOW) + (band // 4) * WINDOW + source // bands
    column = lax.broadcasted_iota(jnp.int32, (taken, order_ref.shape[1]), 1)
    for turn in range(ratio):
        fast = (lax.axis_index("hist") + ratio - turn) % ratio
        hit = column == target + fast * steps % 8
        order_ref[turn * taken : (turn + 1) * taken, :] = jnp.where(hit, 1.0, 0.0).astype(BF16)


def column_kernel(bands, steps, rows, weight, retarded_ref, send_ref, keep_ref, give_ref):
    lanes = 4 * bands
    groups = bands // 4
    hist_start, row_start = (lax.axis_index("hist") * steps, lax.axis_index("row") * rows)
    block = lane_block((bands, lanes), bands)
    later = row_start + lax.broadcasted_iota(jnp.int32, (rows, groups * lanes), 0)
    total = None
    for chunk in range(steps // 4):
        turned = []
        for part in range(2):
            first = (chunk * 4 + 2 + part) * bands
            own = send_ref[first : first + bands, :].astype(F32)
            turned.append([own] + [pltpu.roll(own, d * bands, 1) for d in range(1, 4)])
        for k in range(4):
            step = chunk * 4 + k
            real, imag = [
                jnp.concatenate(
                    [jnp.where(block == b, turned[part][(b - k) % 4], 0.0) for b in range(4)],
                    axis=0,
                )
                for part in range(2)
            ]
            weights = jnp.concatenate(
                [
                    jnp.concatenate([real, imag], axis=1),
                    jnp.concatenate([-imag, real], axis=1),
                ],
                axis=0,
            ).astype(BF16)
            causal = hist_start + step <= later
            halves = []
            for part in range(2):
                whole = jnp.where(causal, retarded_ref[part, step].astype(F32), 0.0)
                halves.append(
                    jnp.concatenate(
                        [whole[:, g * lanes : (g + 1) * lanes] for g in range(groups)], axis=0
                    ).astype(BF16)
                )
            term = lax.dot_general(
                jnp.concatenate(halves, axis=1),
                weights,
                (((1,), (1,)), ((), ())),
                preferred_element_type=F32,
            )
            total = term if total is None else total + term
    low = lax.axis_index("hist") % 2 == 0
    for g in range(groups // 2):
        for part in range(2):
            halves = [
                -weight * total[k * rows : (k + 1) * rows, part * lanes : (part + 1) * lanes]
                for k in (g, g + groups // 2)
            ]
            to = slice((2 * g + part) * rows, (2 * g + part + 1) * rows)
            keep_ref[to, :] = jnp.where(low, halves[0], halves[1])
            give_ref[to, :] = jnp.where(low, halves[1], halves[0])


def add_kernel(own_ref, other_ref, out_ref):
    total = own_ref[...].astype(F32) + other_ref[...].astype(F32)
    out_ref[...] = total.astype(out_ref.dtype)


def final_kernel(count, stepped_ref, own_ref, other_ref, sum_ref, more_ref, row_ref, column_ref):
    squares = (own_ref[...] + other_ref[...])[0:1]
    row_ref[...] = stepped_ref[...] / jnp.sqrt(squares / count + 1e-06)
    low = lax.axis_index("hist") % 2 == 0
    half, back = (sum_ref[...], more_ref[...])
    column = jnp.concatenate([jnp.where(low, half, back), jnp.where(low, back, half)], axis=0)
    rows, lanes = (column_ref.shape[1], column.shape[1])
    for part in range(2):
        for g in range(column_ref.shape[2] // lanes):
            at = (2 * g + part) * rows
            column_ref[part, :, g * lanes : (g + 1) * lanes] = column[at : at + rows]


def row_kernel(bands, steps, rows, weight, ratio, turn, order_ref, lesser_ref, advanced_ref, sent_ref, *refs):
    out_ref = refs[-1]
    lanes = 4 * bands
    groups = bands // 4
    depth = groups * WINDOW
    taken = steps * bands
    fast = (lax.axis_index("hist") + ratio - turn) % ratio
    sigma = jnp.concatenate([sent_ref[c * lanes : (c + 1) * lanes, :] for c in range(steps // 4)], axis=1)
    ordered = jnp.dot(
        sigma,
        order_ref[turn * taken : (turn + 1) * taken, :],
        preferred_element_type=F32,
    )
    lefts = []
    for which in range(2):
        real = ordered[2 * which * bands : (2 * which + 1) * bands]
        imag = ordered[(2 * which + 1) * bands : (2 * which + 2) * bands]
        both = []
        for k in range(4):
            at = slice(k * depth, (k + 1) * depth)
            both.append(jnp.concatenate([real[:, at], -imag[:, at]], axis=1))
            both.append(jnp.concatenate([imag[:, at], real[:, at]], axis=1))
        lefts.append(jnp.concatenate(both, axis=0).astype(BF16))
    starts = [f * steps // 8 * 8 for f in range(ratio)]
    start = fast * steps // 8 * 8
    earlier = lax.axis_index("row") * rows + start
    earlier = earlier + lax.broadcasted_iota(jnp.int32, (WINDOW, groups * lanes), 0)
    hist_start = lax.axis_index("hist") * steps

    def right(which, step):
        ref = (lesser_ref, advanced_ref)[which]
        pieces = []
        for part in range(2):
            whole = ref[part, step].astype(F32)
            window = whole[:WINDOW]
            for f in range(1, ratio):
                window = jnp.where(fast == f, whole[starts[f] : starts[f] + WINDOW], window)
            if which == 1:
                window = jnp.where(earlier <= hist_start + step, window, 0.0)
            pieces += [window[:, g * lanes : (g + 1) * lanes] for g in range(groups)]
        return jnp.concatenate(pieces, axis=0).astype(BF16)

    block = lane_block((2 * bands, lanes), bands)
    sums = []
    for chunk in range(steps // 4):
        gathered = None
        for pair in range(2):
            first = chunk * 4 + pair * 2
            total = None
            for which in range(2):
                rights = jnp.concatenate([right(which, first), right(which, first + 1)], axis=1)
                term = jnp.dot(lefts[which], rights, preferred_element_type=F32)
                total = term if total is None else total + term
            for k in range(2):
                own = total[:, k * lanes : (k + 1) * lanes]
                picked = own[: 2 * bands]
                for b in range(1, 4):
                    picked = jnp.where(block == b, own[2 * bands * b : 2 * bands * (b + 1)], picked)
                picked = picked + pltpu.roll(picked, 2 * bands, 1)
                picked = picked + pltpu.roll(picked, bands, 1)
                gathered = (
                    picked if gathered is None else jnp.where(block == 2 * pair + k, picked, gathered)
                )
        sums.append(weight * gathered)
        if len(refs) > 1:
            sums[-1] = sums[-1] + refs[0][: 2 * bands, chunk * lanes : (chunk + 1) * lanes]
    later = jnp.where(lax.axis_index("row") * ratio + fast > lax.axis_index("hist"), 1.0, 0.0)
    extra = sent_ref[taken:, :bands].astype(F32)
    above_log = later * (extra[0:1] + extra[1:2] + extra[2:3])
    above_phase = later * (extra[3:4] + extra[4:5] + extra[5:6])
    if len(refs) > 1:
        above_log = above_log + refs[0][2 * bands : 2 * bands + 1, :bands]
        above_phase = above_phase + refs[0][2 * bands + 1 : 2 * bands + 2, :bands]
    if turn == 0:
        pack_sum(out_ref, bands, sums, (above_log, above_phase))
        return
    for chunk, part in enumerate(sums):
        out_ref[: 2 * bands, chunk * lanes : (chunk + 1) * lanes] = part
    at = lax.broadcasted_iota(jnp.int32, (8, bands), 0)
    out_ref[2 * bands :, :] = jnp.zeros((8, steps * bands), F32)
    out_ref[2 * bands :, :bands] = jnp.where(at == 0, above_log, jnp.where(at == 1, above_phase, 0.0))


def pieces_of(totals):
    shape = (EXTRA, totals[0].shape[1])
    row = lax.broadcasted_iota(jnp.int32, shape, 0)
    extra = jnp.zeros(shape, F32)
    at = 0
    for total in totals:
        for _ in range(3):
            piece = total.astype(BF16).astype(F32)
            extra = jnp.where(row == at, piece, extra)
            total = total - piece
            at += 1
    return extra


def pack_sum(out_ref, bands, chunks, above):
    last = len(chunks) * 2 * bands
    for k, part in enumerate(chunks):
        out_ref[2 * bands * k : 2 * bands * (k + 1), :] = part.astype(BF16)
    out_ref[last:, :] = jnp.zeros((EXTRA, 4 * bands), BF16)
    out_ref[last:, :bands] = pieces_of(above).astype(BF16)


def unpack_sum(own_ref, other_ref, bands):
    last = own_ref.shape[0] - EXTRA
    total = own_ref[...].astype(F32) + other_ref[...].astype(F32)
    chunks = [total[2 * bands * k : 2 * bands * (k + 1)] for k in range(last // (2 * bands))]
    extra = total[last:, :bands]
    return chunks, (extra[0:1] + extra[1:2] + extra[2:3], extra[3:4] + extra[4:5] + extra[5:6])


def narrow_kernel(bands, own_ref, other_ref, out_ref):
    pack_sum(out_ref, bands, *unpack_sum(own_ref, other_ref, bands))


def step_kernel(
    bands, steps, damping_ref, phases_ref, packed_ref, own_ref, other_ref,
    out_ref, square_ref, work
):
    lanes = 4 * bands
    groups = bands // 4
    chunks, (above_log, above_phase) = unpack_sum(own_ref, other_ref, bands)
    at = lax.broadcasted_iota(jnp.int32, (steps, bands), 0)
    rates = jnp.log(damping_ref[...])
    phases = phases_ref[...]
    summed_log = jnp.broadcast_to(above_log, (steps, bands))
    summed_phase = jnp.broadcast_to(above_phase, (steps, bands))
    for step in range(steps):
        summed_log = summed_log + jnp.where(at <= step, rates[step : step + 1], 0.0)
        summed_phase = summed_phase + jnp.where(at <= step, phases[step : step + 1], 0.0)
    magnitude = jnp.exp(summed_log)
    both = jnp.concatenate(
        [magnitude * jnp.cos(summed_phase), -magnitude * jnp.sin(summed_phase)], axis=1
    )
    wide = lax.broadcasted_iota(jnp.int32, (steps, steps * bands), 1) // bands
    place = lax.broadcasted_iota(jnp.int32, (steps, steps * bands), 0)
    spreading = jnp.where(wide == place, 1.0, 0.0)
    factor = lax.dot_general(
        both, spreading, (((0,), (0,)), ((), ())), precision=HIGHEST, preferred_element_type=F32
    )
    row = packed_ref[...] + jnp.concatenate(chunks, axis=1)
    row_real, row_imag = (row[:bands], row[bands:])
    factor_real, factor_imag = (factor[:bands], factor[bands:])
    stepped = (
        factor_real * row_real - factor_imag * row_imag,
        factor_real * row_imag + factor_imag * row_real,
    )
    squares = jnp.sum(stepped[0] * stepped[0] + stepped[1] * stepped[1], keepdims=True)
    square_ref[...] = jnp.broadcast_to(squares, square_ref.shape)
    for part in range(2):
        for chunk in range(steps // 4):
            work[part, chunk] = stepped[part][:, chunk * lanes : (chunk + 1) * lanes]
    for part in range(2):
        for chunk in range(steps // 4):
            blocks = [work[part, chunk, pl.ds(k, groups, stride=4), :] for k in range(4)]
            for k, block in enumerate(swap_blocks(blocks)):
                first = (chunk * 4 + k) * groups * 2 + part
                out_ref[pl.ds(first, groups, stride=2), :] = block


def call(kernel, shapes, scratch, flops, moved, spaces, *operands):
    return pl.pallas_call(
        kernel,
        out_shape=shapes,
        in_specs=[pl.BlockSpec(memory_space=space) for space in spaces],
        out_specs=[pl.BlockSpec(memory_space=pltpu.VMEM)] * len(shapes),
        scratch_shapes=scratch,
        compiler_params=pltpu.CompilerParams(vmem_limit_bytes=VMEM_LIMIT),
        cost_estimate=pl.CostEstimate(flops=flops, bytes_accessed=moved, transcendentals=0),
    )(*operands)


def shards(
    row_less, row_great, coupling, damping, phases, lesser_hist, advanced_hist, retarded_hist
):
    bands = coupling.shape[0]
    lanes = 4 * bands
    groups = bands // 4
    steps = row_less.shape[1]
    rows = lesser_hist.shape[1]
    hist_count, row_count = (lax.axis_size("hist"), lax.axis_size("row"))
    ratio = hist_count // row_count
    all_steps = steps * hist_count
    weight = float(all_steps * bands) ** (-0.5)
    taken = steps * bands
    sds = jax.ShapeDtypeStruct

    def grouped(x):
        x = x.reshape(2, steps, groups, lanes).transpose(1, 2, 0, 3)
        return x.reshape(steps * groups * 2, lanes)

    retarded = retarded_hist.transpose(0, 2, 1, 3)
    vmem = pltpu.VMEM
    (order,) = call(
        functools.partial(order_kernel, bands, steps, ratio),
        [sds((ratio * taken, bands * WINDOW), BF16)],
        [],
        10**10,
        10**7,
        [],
    )
    send, packed = call(
        functools.partial(energy_kernel, bands, steps),
        [sds((taken + EXTRA, lanes), BF16), sds((2 * bands, taken), F32)],
        [vmem((2, 2, steps // 4 * bands, lanes), F32)],
        10**8,
        10**6,
        [pl.ANY] + [vmem] * 5,
        order,
        grouped(row_less),
        grouped(row_great),
        coupling,
        damping,
        phases,
    )
    arrived = [swap_places(send, turn) for turn in range(ratio)]
    column, give = call(
        functools.partial(column_kernel, bands, steps, rows, weight),
        [sds((groups * rows, lanes), F32)] * 2,
        [],
        10**9,
        4 * 10**6,
        [vmem] * 2,
        retarded,
        send,
    )

    def add(own, other, kind):
        (out,) = call(
            add_kernel, [sds(own.shape, kind)], [], 10**10, 10**6, [vmem] * 2, own, other
        )
        return out

    got = crossed(give, "hist", 1)
    summed = sds((steps // 4 * 2 * bands + EXTRA, lanes), BF16)
    partial_row = []
    for turn in reversed(range(ratio)):
        partial_row = call(
            functools.partial(row_kernel, bands, steps, rows, weight, ratio, turn),
            [summed if turn == 0 else sds((2 * bands + 8, taken), F32)],
            [],
            10**6 if turn == 0 else 10**6,
            10**6,
            [vmem] * (4 + len(partial_row)),
            order,
            lesser_hist.transpose(0, 2, 1, 3),
            advanced_hist.transpose(0, 2, 1, 3),
            arrived[turn],
            *partial_row,
        )
    partial_row = partial_row[0]
    bit = 1
    while 2 * bit < row_count:
        (partial_row,) = call(
            functools.partial(narrow_kernel, bands),
            [summed],
            [],
            10**6,
            10**6,
            [vmem] * 2,
            partial_row,
            crossed(partial_row, "row", bit),
        )
        bit *= 2
    other = crossed(partial_row, "row", bit)
    column = add(column, got, BF16)
    got = crossed(column, "hist", hist_count // 2)
    stepped, squares = call(
        functools.partial(step_kernel, bands, steps),
        [sds((steps * groups * 2, lanes), F32), sds((8, lanes), F32)],
        [vmem((2, steps // 4, bands, lanes), F32)],
        10**10,
        10**6,
        [vmem] * 5,
        damping,
        phases,
        packed,
        partial_row,
        other,
    )
    ahead = [hist_count >> k for k in range(1, hist_count.bit_length() - 1)]
    beside = ahead[1:] + [1, None]
    for bit, each in zip([1] + ahead, beside):
        other = crossed(squares, "hist", bit)
        if each:
            column = add(column, got, BF16 if each == 2 else F32)
            got = crossed(column, "hist", each)
            squares = add(squares, other, F32)
    got, other = lax.optimization_barrier((got, other))
    stepped, column = call(
        functools.partial(final_kernel, float(2 * all_steps * bands * bands)),
        [sds(stepped.shape, F32), sds((2, rows, bands * bands), F32)],
        [],
        10**6,
        10**6,
        [vmem] * 5,
        stepped,
        squares,
        other,
        column,
        got,
    )
    stepped = stepped.reshape(steps, groups, 2, lanes).transpose(2, 0, 1, 3)
    return (stepped.reshape(2, steps, bands * bands), column)


def solution(mesh):
    return jax.shard_map(
        shards,
        mesh=mesh,
        in_specs=(
            P(None, "hist", None),
            P(None, "hist", None),
            P(),
            P("hist", None),
            P("hist", None),
            P(None, "row", "hist", None),
            P(None, "row", "hist", None),
            P(None, "row", "hist", None),
        ),
        out_specs=(P(None, "hist", None), P(None, "row", None)),
        check_vma=False,
    )
```

```python
import functools

import jax
import jax.numpy as jnp
from jax import lax
from jax.experimental import pallas as pl
from jax.experimental.pallas import tpu as pltpu
from jax.sharding import PartitionSpec as P

F32, BF16 = (jnp.float32, jnp.bfloat16)
HIGHEST = lax.Precision.HIGHEST
EXTRA = 16
WINDOW = 16
VMEM_LIMIT = 48 * 1024 * 1024


def swap_places(x, turn):
    hist_count, row_count = (lax.axis_size("hist"), lax.axis_size("row"))
    ratio = hist_count // row_count
    cores = 2 if row_count % 2 == 0 else 1
    span = row_count // cores
    pairs = []
    for slow in range(row_count):
        for fast in range(ratio):
            for row in range(row_count):
                source = (slow * ratio + fast) * row_count + row
                goal = row % cores * span + (row // cores + 1 + turn) % span
                target = (goal * ratio + (fast + turn) % ratio) * row_count + slow
                pairs.append((source, target))
    return lax.ppermute(x, ("hist", "row"), pairs)


def crossed(x, axis, bit):
    size = lax.axis_size(axis)
    return lax.ppermute(x, axis, [(k, k ^ bit) for k in range(size)])


def lane_block(shape, width):
    return lax.broadcasted_iota(jnp.int32, shape, len(shape) - 1) // width


def swap_blocks(parts):
    width = parts[0].shape[1] // 4
    block = lane_block(parts[0].shape, width)
    parts = list(parts)
    for bit in (2, 1):
        new = list(parts)
        for a in range(4):
            if a & bit == 0:
                low, high = (parts[a], parts[a | bit])
                shift = bit * width
                keep = block & bit == 0
                new[a] = jnp.where(keep, low, pltpu.roll(high, shift, 1))
                new[a | bit] = jnp.where(keep, pltpu.roll(low, 4 * width - shift, 1), high)
        parts = new
    return parts


def split_dot(left, right, dims):
    highs = [x.astype(BF16) for x in (left, right)]
    lows = [(x - high.astype(F32)).astype(BF16) for x, high in zip((left, right), highs)]

    def product(a, b):
        return lax.dot_general(a, b, dims, preferred_element_type=F32)

    return product(highs[0], highs[1]) + (product(highs[0], lows[1]) + product(lows[0], highs[1]))


def energy_kernel(bands, steps, order_ref, less_ref, great_ref, coupling_ref, damping_ref, phases_ref, send_ref, packed_ref, work):
    groups = bands // 4
    chunks = steps // 4
    for which, ref in enumerate((less_ref, great_ref)):
        for part in range(2):
            for chunk in range(chunks):
                blocks = [
                    ref[pl.ds((chunk * 4 + k) * groups * 2 + part, groups, stride=2), :]
                    for k in range(4)
                ]
                for k, block in enumerate(swap_blocks(blocks)):
                    work[which, part, pl.ds(chunk * bands + k, groups, stride=4), :] = block
    less_real, less_imag = (work[0, 0], work[0, 1])
    great_real, great_imag = (work[1, 0], work[1, 1])
    polar = jnp.concatenate(
        [
            -(less_real * great_real + less_imag * great_imag),
            -(less_imag * great_real - less_real * great_imag),
        ],
        axis=0,
    )
    coupling = coupling_ref[...]
    wide = jnp.concatenate([coupling] * 4, axis=1)
    tall = jnp.concatenate([wide] * 4, axis=0)
    at_row = lax.broadcasted_iota(jnp.int32, tall.shape, 0) // bands
    blocked = jnp.where(at_row == lane_block(tall.shape, bands), tall, 0.0)
    half = split_dot(polar, blocked, (((1,), (1,)), ((), ())))
    rows = chunks * bands
    both = jnp.concatenate([half[:rows], half[rows:]], axis=1)
    screens = []
    for chunk in range(chunks):
        part = both[chunk * bands : (chunk + 1) * bands]
        screens.append(split_dot(coupling, part, (((1,), (0,)), ((), ()))))
    screen = jnp.concatenate(screens, axis=0)
    lanes = 4 * bands
    screen_real, screen_imag = (screen[:, :lanes], screen[:, lanes:])
    sigma_real = less_real * screen_real - less_imag * screen_imag
    sigma_imag = less_real * screen_imag + less_imag * screen_real
    wide_real = great_real * screen_real + great_imag * screen_imag
    wide_imag = great_imag * screen_real - great_real * screen_imag
    outs = (wide_real - sigma_real, wide_imag - sigma_imag, sigma_real, sigma_imag)
    for chunk in range(chunks):
        at = slice(chunk * bands, (chunk + 1) * bands)
        to = slice(chunk * lanes, (chunk + 1) * lanes)
        for k, out in enumerate(outs):
            first = (chunk * 4 + k) * bands
            send_ref[first : first + bands, :] = out[at].astype(BF16)
        packed_ref[:bands, to] = less_real[at]
        packed_ref[bands:, to] = less_imag[at]
    log_total = jnp.sum(jnp.log(damping_ref[...]), axis=0, keepdims=True)
    phase_total = jnp.sum(phases_ref[...], axis=0, keepdims=True)
    last = steps * bands
    send_ref[last:, :] = jnp.zeros((EXTRA, lanes), BF16)
    send_ref[last:, :bands] = pieces_of((log_total, phase_total)).astype(BF16)


def order_kernel(bands, steps, ratio, order_ref):
    groups = bands // 4
    taken = steps * bands
    source = lax.broadcasted_iota(jnp.int32, (taken, 1), 0)
    band = source % bands
    target = (band % 4) * (groups * WINDOW) + (band // 4) * WINDOW + source // bands
    column = lax.broadcasted_iota(jnp.int32, (taken, order_ref.shape[1]), 1)
    for turn in range(ratio):
        fast = (lax.axis_index("hist") + ratio - turn) % ratio
        hit = column == target + fast * steps % 8
        order_ref[turn * taken : (turn + 1) * taken, :] = jnp.where(hit, 1.0, 0.0).astype(BF16)


def column_kernel(bands, steps, rows, weight, retarded_ref, send_ref, keep_ref, give_ref):
    lanes = 4 * bands
    groups = bands // 4
    hist_start, row_start = (lax.axis_index("hist") * steps, lax.axis_index("row") * rows)
    block = lane_block((bands, lanes), bands)
    later = row_start + lax.broadcasted_iota(jnp.int32, (rows, groups * lanes), 0)
    total = None
    for chunk in range(steps // 4):
        turned = []
        for part in range(2):
            first = (chunk * 4 + 2 + part) * bands
            own = send_ref[first : first + bands, :].astype(F32)
            turned.append([own] + [pltpu.roll(own, d * bands, 1) for d in range(1, 4)])
        for k in range(4):
            step = chunk * 4 + k
            real, imag = [
                jnp.concatenate(
                    [jnp.where(block == b, turned[part][(b - k) % 4], 0.0) for b in range(4)],
                    axis=0,
                )
                for part in range(2)
            ]
            weights = jnp.concatenate(
                [
                    jnp.concatenate([real, imag], axis=1),
                    jnp.concatenate([-imag, real], axis=1),
                ],
                axis=0,
            ).astype(BF16)
            causal = hist_start + step <= later
            halves = []
            for part in range(2):
                whole = jnp.where(causal, retarded_ref[part, step].astype(F32), 0.0)
                halves.append(
                    jnp.concatenate(
                        [whole[:, g * lanes : (g + 1) * lanes] for g in range(groups)], axis=0
                    ).astype(BF16)
                )
            term = lax.dot_general(
                jnp.concatenate(halves, axis=1),
                weights,
                (((1,), (1,)), ((), ())),
                preferred_element_type=F32,
            )
            total = term if total is None else total + term
    low = lax.axis_index("hist") % 2 == 0
    give_ref[groups * rows :, :] = jnp.zeros((give_ref.shape[0] - groups * rows, lanes), BF16)
    for g in range(groups // 2):
        for part in range(2):
            halves = [
                -weight * total[k * rows : (k + 1) * rows, part * lanes : (part + 1) * lanes]
                for k in (g, g + groups // 2)
            ]
            to = slice((2 * g + part) * rows, (2 * g + part + 1) * rows)
            keep_ref[to, :] = jnp.where(low, halves[0], halves[1])
            give_ref[to, :] = jnp.where(low, halves[1], halves[0]).astype(BF16)


def add_kernel(own_ref, other_ref, out_ref):
    total = own_ref[...].astype(F32) + other_ref[: own_ref.shape[0], :].astype(F32)
    out_ref[...] = total.astype(out_ref.dtype)


def final_kernel(count, stepped_ref, own_ref, other_ref, sum_ref, more_ref, row_ref, column_ref):
    squares = (own_ref[...] + other_ref[...])[0:1]
    row_ref[...] = stepped_ref[...] / jnp.sqrt(squares / count + 1e-06)
    low = lax.axis_index("hist") % 2 == 0
    half, back = (sum_ref[...], more_ref[...])
    column = jnp.concatenate([jnp.where(low, half, back), jnp.where(low, back, half)], axis=0)
    rows, lanes = (column_ref.shape[1], column.shape[1])
    for part in range(2):
        for g in range(column_ref.shape[2] // lanes):
            at = (2 * g + part) * rows
            column_ref[part, :, g * lanes : (g + 1) * lanes] = column[at : at + rows]


def right_operand(bands, steps, rows, ratio, turn, lesser_ref, advanced_ref):
    lanes = 4 * bands
    groups = bands // 4
    fast = (lax.axis_index("hist") + ratio - turn) % ratio
    starts = [f * steps // 8 * 8 for f in range(ratio)]
    start = fast * steps // 8 * 8
    earlier = lax.axis_index("row") * rows + start
    earlier = earlier + lax.broadcasted_iota(jnp.int32, (WINDOW, groups * lanes), 0)
    hist_start = lax.axis_index("hist") * steps

    def right(which, step):
        ref = (lesser_ref, advanced_ref)[which]
        pieces = []
        for part in range(2):
            whole = ref[part, step].astype(F32)
            window = whole[:WINDOW]
            for f in range(1, ratio):
                window = jnp.where(fast == f, whole[starts[f] : starts[f] + WINDOW], window)
            if which == 1:
                window = jnp.where(earlier <= hist_start + step, window, 0.0)
            pieces += [window[:, g * lanes : (g + 1) * lanes] for g in range(groups)]
        return jnp.concatenate(pieces, axis=0).astype(BF16)

    return right


def right_kernel(bands, steps, rows, ratio, turn, lesser_ref, advanced_ref, out_ref):
    right = right_operand(bands, steps, rows, ratio, turn, lesser_ref, advanced_ref)
    depth = 2 * bands // 4 * WINDOW
    for which in range(2):
        for pair in range(steps // 2):
            at = (which * steps // 2 + pair) * depth
            both = [right(which, 2 * pair), right(which, 2 * pair + 1)]
            out_ref[at : at + depth, :] = jnp.concatenate(both, axis=1)


def row_kernel(bands, steps, rows, weight, ratio, turn, order_ref, lesser_ref, advanced_ref, sent_ref, *refs):
    out_ref = refs[-1]
    lanes = 4 * bands
    groups = bands // 4
    depth = groups * WINDOW
    taken = steps * bands
    fast = (lax.axis_index("hist") + ratio - turn) % ratio
    sigma = jnp.concatenate([sent_ref[c * lanes : (c + 1) * lanes, :] for c in range(steps // 4)], axis=1)
    ordered = jnp.dot(
        sigma,
        order_ref[turn * taken : (turn + 1) * taken, :],
        preferred_element_type=F32,
    )
    lefts = []
    for which in range(2):
        real = ordered[2 * which * bands : (2 * which + 1) * bands]
        imag = ordered[(2 * which + 1) * bands : (2 * which + 2) * bands]
        both = []
        for k in range(4):
            at = slice(k * depth, (k + 1) * depth)
            both.append(jnp.concatenate([real[:, at], -imag[:, at]], axis=1))
            both.append(jnp.concatenate([imag[:, at], real[:, at]], axis=1))
        lefts.append(jnp.concatenate(both, axis=0).astype(BF16))
    built = len(lesser_ref.shape) == 2
    if not built:
        right = right_operand(bands, steps, rows, ratio, turn, lesser_ref, advanced_ref)

    block = lane_block((2 * bands, lanes), bands)
    sums = []
    for chunk in range(steps // 4):
        gathered = None
        for pair in range(2):
            first = chunk * 4 + pair * 2
            total = None
            for which in range(2):
                if built:
                    at = (which * steps // 2 + first // 2) * 2 * depth
                    rights = lesser_ref[at : at + 2 * depth, :]
                else:
                    rights = jnp.concatenate([right(which, first), right(which, first + 1)], axis=1)
                term = jnp.dot(lefts[which], rights, preferred_element_type=F32)
                total = term if total is None else total + term
            for k in range(2):
                own = total[:, k * lanes : (k + 1) * lanes]
                picked = own[: 2 * bands]
                for b in range(1, 4):
                    picked = jnp.where(block == b, own[2 * bands * b : 2 * bands * (b + 1)], picked)
                picked = picked + pltpu.roll(picked, 2 * bands, 1)
                picked = picked + pltpu.roll(picked, bands, 1)
                gathered = (
                    picked if gathered is None else jnp.where(block == 2 * pair + k, picked, gathered)
                )
        sums.append(weight * gathered)
        if len(refs) > 1:
            sums[-1] = sums[-1] + refs[0][: 2 * bands, chunk * lanes : (chunk + 1) * lanes]
    later = jnp.where(lax.axis_index("row") * ratio + fast > lax.axis_index("hist"), 1.0, 0.0)
    extra = sent_ref[taken:, :bands].astype(F32)
    above_log = later * (extra[0:1] + extra[1:2] + extra[2:3])
    above_phase = later * (extra[3:4] + extra[4:5] + extra[5:6])
    if len(refs) > 1:
        above_log = above_log + refs[0][2 * bands : 2 * bands + 1, :bands]
        above_phase = above_phase + refs[0][2 * bands + 1 : 2 * bands + 2, :bands]
    if turn == 0:
        pack_sum(out_ref, bands, sums, (above_log, above_phase))
        return
    for chunk, part in enumerate(sums):
        out_ref[: 2 * bands, chunk * lanes : (chunk + 1) * lanes] = part
    at = lax.broadcasted_iota(jnp.int32, (8, bands), 0)
    out_ref[2 * bands :, :] = jnp.zeros((8, steps * bands), F32)
    out_ref[2 * bands :, :bands] = jnp.where(at == 0, above_log, jnp.where(at == 1, above_phase, 0.0))


def pieces_of(totals):
    shape = (EXTRA, totals[0].shape[1])
    row = lax.broadcasted_iota(jnp.int32, shape, 0)
    extra = jnp.zeros(shape, F32)
    at = 0
    for total in totals:
        for _ in range(3):
            piece = total.astype(BF16).astype(F32)
            extra = jnp.where(row == at, piece, extra)
            total = total - piece
            at += 1
    return extra


def pack_sum(out_ref, bands, chunks, above):
    last = len(chunks) * 2 * bands
    for k, part in enumerate(chunks):
        out_ref[2 * bands * k : 2 * bands * (k + 1), :] = part.astype(BF16)
    out_ref[last:, :] = jnp.zeros((EXTRA, 4 * bands), BF16)
    out_ref[last:, :bands] = pieces_of(above).astype(BF16)


def unpack_sum(own_ref, other_ref, bands):
    last = own_ref.shape[0] - EXTRA
    total = own_ref[...].astype(F32) + other_ref[...].astype(F32)
    chunks = [total[2 * bands * k : 2 * bands * (k + 1)] for k in range(last // (2 * bands))]
    extra = total[last:, :bands]
    return chunks, (extra[0:1] + extra[1:2] + extra[2:3], extra[3:4] + extra[4:5] + extra[5:6])


def narrow_kernel(bands, own_ref, other_ref, out_ref):
    pack_sum(out_ref, bands, *unpack_sum(own_ref, other_ref, bands))


def step_kernel(
    bands, steps, damping_ref, phases_ref, packed_ref, own_ref, other_ref,
    out_ref, square_ref
):
    lanes = 4 * bands
    groups = bands // 4
    chunks, (above_log, above_phase) = unpack_sum(own_ref, other_ref, bands)
    at = lax.broadcasted_iota(jnp.int32, (steps, bands), 0)
    rates = jnp.log(damping_ref[...])
    phases = phases_ref[...]
    summed_log = jnp.broadcast_to(above_log, (steps, bands))
    summed_phase = jnp.broadcast_to(above_phase, (steps, bands))
    for step in range(steps):
        summed_log = summed_log + jnp.where(at <= step, rates[step : step + 1], 0.0)
        summed_phase = summed_phase + jnp.where(at <= step, phases[step : step + 1], 0.0)
    magnitude = jnp.exp(summed_log)
    both = jnp.concatenate(
        [magnitude * jnp.cos(summed_phase), -magnitude * jnp.sin(summed_phase)], axis=1
    )
    wide = lax.broadcasted_iota(jnp.int32, (steps, steps * bands), 1) // bands
    place = lax.broadcasted_iota(jnp.int32, (steps, steps * bands), 0)
    spreading = jnp.where(wide == place, 1.0, 0.0)
    factor = lax.dot_general(
        both, spreading, (((0,), (0,)), ((), ())), precision=HIGHEST, preferred_element_type=F32
    )
    row = packed_ref[...] + jnp.concatenate(chunks, axis=1)
    row_real, row_imag = (row[:bands], row[bands:])
    factor_real, factor_imag = (factor[:bands], factor[bands:])
    stepped = (
        factor_real * row_real - factor_imag * row_imag,
        factor_real * row_imag + factor_imag * row_real,
    )
    squares = jnp.sum(stepped[0] * stepped[0] + stepped[1] * stepped[1], keepdims=True)
    square_ref[...] = jnp.broadcast_to(squares, square_ref.shape)
    out_ref[:bands, :] = stepped[0]
    out_ref[bands:, :] = stepped[1]


def relayout_kernel(bands, steps, stepped_ref, out_ref, work):
    lanes = 4 * bands
    groups = bands // 4
    for part in range(2):
        for chunk in range(steps // 4):
            work[part, chunk] = stepped_ref[
                part * bands : (part + 1) * bands, chunk * lanes : (chunk + 1) * lanes
            ]
    for part in range(2):
        for chunk in range(steps // 4):
            blocks = [work[part, chunk, pl.ds(k, groups, stride=4), :] for k in range(4)]
            for k, block in enumerate(swap_blocks(blocks)):
                first = (chunk * 4 + k) * groups * 2 + part
                out_ref[pl.ds(first, groups, stride=2), :] = block


def call(kernel, shapes, scratch, flops, moved, spaces, *operands):
    return pl.pallas_call(
        kernel,
        out_shape=shapes,
        in_specs=[pl.BlockSpec(memory_space=space) for space in spaces],
        out_specs=[pl.BlockSpec(memory_space=pltpu.VMEM)] * len(shapes),
        scratch_shapes=scratch,
        compiler_params=pltpu.CompilerParams(vmem_limit_bytes=VMEM_LIMIT),
        cost_estimate=pl.CostEstimate(flops=flops, bytes_accessed=moved, transcendentals=0),
    )(*operands)


def shards(
    row_less, row_great, coupling, damping, phases, lesser_hist, advanced_hist, retarded_hist
):
    bands = coupling.shape[0]
    lanes = 4 * bands
    groups = bands // 4
    steps = row_less.shape[1]
    rows = lesser_hist.shape[1]
    hist_count, row_count = (lax.axis_size("hist"), lax.axis_size("row"))
    ratio = hist_count // row_count
    all_steps = steps * hist_count
    weight = float(all_steps * bands) ** (-0.5)
    taken = steps * bands
    sds = jax.ShapeDtypeStruct

    def grouped(x):
        x = x.reshape(2, steps, groups, lanes).transpose(1, 2, 0, 3)
        return x.reshape(steps * groups * 2, lanes)

    retarded = retarded_hist.transpose(0, 2, 1, 3)
    vmem = pltpu.VMEM
    (order,) = call(
        functools.partial(order_kernel, bands, steps, ratio),
        [sds((ratio * taken, bands * WINDOW), BF16)],
        [],
        10**10,
        10**7,
        [],
    )
    send, packed = call(
        functools.partial(energy_kernel, bands, steps),
        [sds((taken + EXTRA, lanes), BF16), sds((2 * bands, taken), F32)],
        [vmem((2, 2, steps // 4 * bands, lanes), F32)],
        10**8,
        10**6,
        [pl.ANY] + [vmem] * 5,
        order,
        grouped(row_less),
        grouped(row_great),
        coupling,
        damping,
        phases,
    )
    arrived = [swap_places(send, turn) for turn in range(ratio)]
    column, give = call(
        functools.partial(column_kernel, bands, steps, rows, weight),
        [sds((groups * rows, lanes), F32), sds((groups * rows + 2 * EXTRA, lanes), BF16)],
        [],
        10**9,
        4 * 10**6,
        [vmem] * 2,
        retarded,
        send,
    )

    def add(own, other, kind):
        (out,) = call(
            add_kernel, [sds(own.shape, kind)], [], 10**10, 10**6, [vmem] * 2, own, other
        )
        return out

    got = crossed(give, "hist", 1)
    summed = sds((steps // 4 * 2 * bands + EXTRA, lanes), BF16)
    histories = [lesser_hist.transpose(0, 2, 1, 3), advanced_hist.transpose(0, 2, 1, 3)]
    (rights,) = call(
        functools.partial(right_kernel, bands, steps, rows, ratio, 0),
        [sds((steps * 2 * bands // 4 * WINDOW, 2 * lanes), BF16)],
        [],
        10**4,
        10**4,
        [vmem] * 2,
        *histories,
    )
    order_first, rights = lax.optimization_barrier((order, rights))
    partial_row = []
    for turn in reversed(range(ratio)):
        operands = [order_first] + histories if turn else [order, rights, rights]
        operands += [arrived[turn], *partial_row]
        partial_row = call(
            functools.partial(row_kernel, bands, steps, rows, weight, ratio, turn),
            [summed if turn == 0 else sds((2 * bands + 8, taken), F32)],
            [],
            10**4,
            10**4,
            [vmem] * len(operands),
            *operands,
        )
    partial_row = partial_row[0]
    bit = 1
    while 2 * bit < row_count:
        (partial_row,) = call(
            functools.partial(narrow_kernel, bands),
            [summed],
            [],
            10**4,
            10**4,
            [vmem] * 2,
            partial_row,
            crossed(partial_row, "row", bit),
        )
        bit *= 2
    other = crossed(partial_row, "row", bit)
    column = add(column, got, BF16)
    got = crossed(column, "hist", hist_count // 2)
    stepped, squares = call(
        functools.partial(step_kernel, bands, steps),
        [sds((2 * bands, taken), F32), sds((8, lanes), F32)],
        [],
        10**10,
        10**6,
        [vmem] * 5,
        damping,
        phases,
        packed,
        partial_row,
        other,
    )
    (stepped,) = call(
        functools.partial(relayout_kernel, bands, steps),
        [sds((steps * groups * 2, lanes), F32)],
        [vmem((2, steps // 4, bands, lanes), F32)],
        10**10,
        10**6,
        [vmem],
        stepped,
    )
    ahead = [hist_count >> k for k in range(1, hist_count.bit_length() - 1)]
    beside = ahead[1:] + [1, None]
    for bit, each in zip([1] + ahead, beside):
        other = crossed(squares, "hist", bit)
        if each:
            column = add(column, got, F32)
            got = crossed(column, "hist", each)
            squares = add(squares, other, F32)
    got, other = lax.optimization_barrier((got, other))
    stepped, column = call(
        functools.partial(final_kernel, float(2 * all_steps * bands * bands)),
        [sds(stepped.shape, F32), sds((2, rows, bands * bands), F32)],
        [],
        10**6,
        10**6,
        [vmem] * 5,
        stepped,
        squares,
        other,
        column,
        got,
    )
    stepped = stepped.reshape(steps, groups, 2, lanes).transpose(2, 0, 1, 3)
    return (stepped.reshape(2, steps, bands * bands), column)


def solution(mesh):
    return jax.shard_map(
        shards,
        mesh=mesh,
        in_specs=(
            P(None, "hist", None),
            P(None, "hist", None),
            P(),
            P("hist", None),
            P("hist", None),
            P(None, "row", "hist", None),
            P(None, "row", "hist", None),
            P(None, "row", "hist", None),
        ),
        out_specs=(P(None, "hist", None), P(None, "row", None)),
        check_vma=False,
    )
```

```python
import functools

import jax
import jax.numpy as jnp
from jax import lax
from jax.experimental import pallas as pl
from jax.experimental.pallas import tpu as pltpu
from jax.sharding import PartitionSpec as P

F32, BF16 = (jnp.float32, jnp.bfloat16)
HIGHEST = lax.Precision.HIGHEST
EXTRA = 16
WINDOW = 16
VMEM_LIMIT = 48 * 1024 * 1024


def swap_places(x, turn):
    hist_count, row_count = (lax.axis_size("hist"), lax.axis_size("row"))
    ratio = hist_count // row_count
    cores = 2 if row_count % 2 == 0 else 1
    span = row_count // cores
    pairs = []
    for slow in range(row_count):
        for fast in range(ratio):
            for row in range(row_count):
                source = (slow * ratio + fast) * row_count + row
                shift = turn + (1 if slow in (0, row_count - 1) else 0)
                goal = row % cores * span + (row // cores + shift) % span
                target = (goal * ratio + (fast + turn) % ratio) * row_count + slow
                pairs.append((source, target))
    return lax.ppermute(x, ("hist", "row"), pairs)


def crossed(x, axis, bit):
    size = lax.axis_size(axis)
    return lax.ppermute(x, axis, [(k, k ^ bit) for k in range(size)])


def lane_block(shape, width):
    return lax.broadcasted_iota(jnp.int32, shape, len(shape) - 1) // width


def swap_blocks(parts):
    width = parts[0].shape[1] // 4
    block = lane_block(parts[0].shape, width)
    parts = list(parts)
    for bit in (2, 1):
        new = list(parts)
        for a in range(4):
            if a & bit == 0:
                low, high = (parts[a], parts[a | bit])
                shift = bit * width
                keep = block & bit == 0
                new[a] = jnp.where(keep, low, pltpu.roll(high, shift, 1))
                new[a | bit] = jnp.where(keep, pltpu.roll(low, 4 * width - shift, 1), high)
        parts = new
    return parts


def split_dot(left, right, dims):
    highs = [x.astype(BF16) for x in (left, right)]
    lows = [(x - high.astype(F32)).astype(BF16) for x, high in zip((left, right), highs)]

    def product(a, b):
        return lax.dot_general(a, b, dims, preferred_element_type=F32)

    return product(highs[0], highs[1]) + (product(highs[0], lows[1]) + product(lows[0], highs[1]))


def energy_kernel(bands, steps, order_ref, less_ref, great_ref, coupling_ref, damping_ref, phases_ref, send_ref, packed_ref, work):
    groups = bands // 4
    chunks = steps // 4
    for which, ref in enumerate((less_ref, great_ref)):
        for part in range(2):
            for chunk in range(chunks):
                blocks = [
                    ref[pl.ds((chunk * 4 + k) * groups * 2 + part, groups, stride=2), :]
                    for k in range(4)
                ]
                for k, block in enumerate(swap_blocks(blocks)):
                    work[which, part, pl.ds(chunk * bands + k, groups, stride=4), :] = block
    less_real, less_imag = (work[0, 0], work[0, 1])
    great_real, great_imag = (work[1, 0], work[1, 1])
    polar = jnp.concatenate(
        [
            -(less_real * great_real + less_imag * great_imag),
            -(less_imag * great_real - less_real * great_imag),
        ],
        axis=0,
    )
    coupling = coupling_ref[...]
    wide = jnp.concatenate([coupling] * 4, axis=1)
    tall = jnp.concatenate([wide] * 4, axis=0)
    at_row = lax.broadcasted_iota(jnp.int32, tall.shape, 0) // bands
    blocked = jnp.where(at_row == lane_block(tall.shape, bands), tall, 0.0)
    half = split_dot(polar, blocked, (((1,), (1,)), ((), ())))
    rows = chunks * bands
    both = jnp.concatenate([half[:rows], half[rows:]], axis=1)
    screens = []
    for chunk in range(chunks):
        part = both[chunk * bands : (chunk + 1) * bands]
        screens.append(split_dot(coupling, part, (((1,), (0,)), ((), ()))))
    screen = jnp.concatenate(screens, axis=0)
    lanes = 4 * bands
    screen_real, screen_imag = (screen[:, :lanes], screen[:, lanes:])
    sigma_real = less_real * screen_real - less_imag * screen_imag
    sigma_imag = less_real * screen_imag + less_imag * screen_real
    wide_real = great_real * screen_real + great_imag * screen_imag
    wide_imag = great_imag * screen_real - great_real * screen_imag
    outs = (wide_real - sigma_real, wide_imag - sigma_imag, sigma_real, sigma_imag)
    for chunk in range(chunks):
        at = slice(chunk * bands, (chunk + 1) * bands)
        to = slice(chunk * lanes, (chunk + 1) * lanes)
        for k, out in enumerate(outs):
            first = (chunk * 4 + k) * bands
            send_ref[first : first + bands, :] = out[at].astype(BF16)
        packed_ref[:bands, to] = less_real[at]
        packed_ref[bands:, to] = less_imag[at]
    log_total = jnp.sum(jnp.log(damping_ref[...]), axis=0, keepdims=True)
    phase_total = jnp.sum(phases_ref[...], axis=0, keepdims=True)
    last = steps * bands
    send_ref[last:, :] = jnp.zeros((EXTRA, lanes), BF16)
    send_ref[last:, :bands] = pieces_of((log_total, phase_total)).astype(BF16)


def order_kernel(bands, steps, ratio, order_ref):
    groups = bands // 4
    taken = steps * bands
    source = lax.broadcasted_iota(jnp.int32, (taken, 1), 0)
    band = source % bands
    target = (band % 4) * (groups * WINDOW) + (band // 4) * WINDOW + source // bands
    column = lax.broadcasted_iota(jnp.int32, (taken, order_ref.shape[1]), 1)
    for turn in range(ratio):
        fast = (lax.axis_index("hist") + ratio - turn) % ratio
        hit = column == target + fast * steps % 8
        order_ref[turn * taken : (turn + 1) * taken, :] = jnp.where(hit, 1.0, 0.0).astype(BF16)


def column_kernel(bands, steps, rows, weight, retarded_ref, send_ref, keep_ref, give_ref):
    lanes = 4 * bands
    groups = bands // 4
    hist_start, row_start = (lax.axis_index("hist") * steps, lax.axis_index("row") * rows)
    block = lane_block((bands, lanes), bands)
    later = row_start + lax.broadcasted_iota(jnp.int32, (rows, groups * lanes), 0)
    total = None
    for chunk in range(steps // 4):
        turned = []
        for part in range(2):
            first = (chunk * 4 + 2 + part) * bands
            own = send_ref[first : first + bands, :].astype(F32)
            turned.append([own] + [pltpu.roll(own, d * bands, 1) for d in range(1, 4)])
        for k in range(4):
            step = chunk * 4 + k
            real, imag = [
                jnp.concatenate(
                    [jnp.where(block == b, turned[part][(b - k) % 4], 0.0) for b in range(4)],
                    axis=0,
                )
                for part in range(2)
            ]
            weights = jnp.concatenate(
                [
                    jnp.concatenate([real, imag], axis=1),
                    jnp.concatenate([-imag, real], axis=1),
                ],
                axis=0,
            ).astype(BF16)
            causal = hist_start + step <= later
            halves = []
            for part in range(2):
                whole = jnp.where(causal, retarded_ref[part, step].astype(F32), 0.0)
                halves.append(
                    jnp.concatenate(
                        [whole[:, g * lanes : (g + 1) * lanes] for g in range(groups)], axis=0
                    ).astype(BF16)
                )
            term = lax.dot_general(
                jnp.concatenate(halves, axis=1),
                weights,
                (((1,), (1,)), ((), ())),
                preferred_element_type=F32,
            )
            total = term if total is None else total + term
    low = lax.axis_index("hist") % 2 == 0
    give_ref[groups * rows :, :] = jnp.zeros((give_ref.shape[0] - groups * rows, lanes), BF16)
    for g in range(groups // 2):
        for part in range(2):
            halves = [
                -weight * total[k * rows : (k + 1) * rows, part * lanes : (part + 1) * lanes]
                for k in (g, g + groups // 2)
            ]
            to = slice((2 * g + part) * rows, (2 * g + part + 1) * rows)
            keep_ref[to, :] = jnp.where(low, halves[0], halves[1])
            give_ref[to, :] = jnp.where(low, halves[1], halves[0]).astype(BF16)


def add_kernel(own_ref, other_ref, out_ref):
    total = own_ref[...].astype(F32) + other_ref[: own_ref.shape[0], :].astype(F32)
    out_ref[...] = total.astype(out_ref.dtype)


def final_kernel(count, stepped_ref, own_ref, other_ref, sum_ref, more_ref, row_ref, column_ref):
    squares = (own_ref[...] + other_ref[...])[0:1]
    row_ref[...] = stepped_ref[...] / jnp.sqrt(squares / count + 1e-06)
    low = lax.axis_index("hist") % 2 == 0
    half, back = (sum_ref[...], more_ref[...])
    column = jnp.concatenate([jnp.where(low, half, back), jnp.where(low, back, half)], axis=0)
    rows, lanes = (column_ref.shape[1], column.shape[1])
    for part in range(2):
        for g in range(column_ref.shape[2] // lanes):
            at = (2 * g + part) * rows
            column_ref[part, :, g * lanes : (g + 1) * lanes] = column[at : at + rows]


def right_operand(bands, steps, rows, ratio, turn, lesser_ref, advanced_ref):
    lanes = 4 * bands
    groups = bands // 4
    fast = (lax.axis_index("hist") + ratio - turn) % ratio
    starts = [f * steps // 8 * 8 for f in range(ratio)]
    start = fast * steps // 8 * 8
    earlier = lax.axis_index("row") * rows + start
    earlier = earlier + lax.broadcasted_iota(jnp.int32, (WINDOW, groups * lanes), 0)
    hist_start = lax.axis_index("hist") * steps

    def right(which, step):
        ref = (lesser_ref, advanced_ref)[which]
        pieces = []
        for part in range(2):
            whole = ref[part, step].astype(F32)
            window = whole[:WINDOW]
            for f in range(1, ratio):
                window = jnp.where(fast == f, whole[starts[f] : starts[f] + WINDOW], window)
            if which == 1:
                window = jnp.where(earlier <= hist_start + step, window, 0.0)
            pieces += [window[:, g * lanes : (g + 1) * lanes] for g in range(groups)]
        return jnp.concatenate(pieces, axis=0).astype(BF16)

    return right


def right_kernel(bands, steps, rows, ratio, turn, lesser_ref, advanced_ref, out_ref):
    right = right_operand(bands, steps, rows, ratio, turn, lesser_ref, advanced_ref)
    depth = 2 * bands // 4 * WINDOW
    for which in range(2):
        for pair in range(steps // 2):
            at = (which * steps // 2 + pair) * depth
            both = [right(which, 2 * pair), right(which, 2 * pair + 1)]
            out_ref[at : at + depth, :] = jnp.concatenate(both, axis=1)


def row_kernel(bands, steps, rows, weight, ratio, turn, order_ref, lesser_ref, advanced_ref, sent_ref, *refs):
    out_ref = refs[-1]
    lanes = 4 * bands
    groups = bands // 4
    depth = groups * WINDOW
    taken = steps * bands
    fast = (lax.axis_index("hist") + ratio - turn) % ratio
    sigma = jnp.concatenate([sent_ref[c * lanes : (c + 1) * lanes, :] for c in range(steps // 4)], axis=1)
    ordered = jnp.dot(
        sigma,
        order_ref[turn * taken : (turn + 1) * taken, :],
        preferred_element_type=F32,
    )
    lefts = []
    for which in range(2):
        real = ordered[2 * which * bands : (2 * which + 1) * bands]
        imag = ordered[(2 * which + 1) * bands : (2 * which + 2) * bands]
        both = []
        for k in range(4):
            at = slice(k * depth, (k + 1) * depth)
            both.append(jnp.concatenate([real[:, at], -imag[:, at]], axis=1))
            both.append(jnp.concatenate([imag[:, at], real[:, at]], axis=1))
        lefts.append(jnp.concatenate(both, axis=0).astype(BF16))
    built = len(lesser_ref.shape) == 2
    if not built:
        right = right_operand(bands, steps, rows, ratio, turn, lesser_ref, advanced_ref)

    block = lane_block((2 * bands, lanes), bands)
    sums = []
    for chunk in range(steps // 4):
        gathered = None
        for pair in range(2):
            first = chunk * 4 + pair * 2
            total = None
            for which in range(2):
                if built:
                    at = (which * steps // 2 + first // 2) * 2 * depth
                    rights = lesser_ref[at : at + 2 * depth, :]
                else:
                    rights = jnp.concatenate([right(which, first), right(which, first + 1)], axis=1)
                term = jnp.dot(lefts[which], rights, preferred_element_type=F32)
                total = term if total is None else total + term
            for k in range(2):
                own = total[:, k * lanes : (k + 1) * lanes]
                picked = own[: 2 * bands]
                for b in range(1, 4):
                    picked = jnp.where(block == b, own[2 * bands * b : 2 * bands * (b + 1)], picked)
                picked = picked + pltpu.roll(picked, 2 * bands, 1)
                picked = picked + pltpu.roll(picked, bands, 1)
                gathered = (
                    picked if gathered is None else jnp.where(block == 2 * pair + k, picked, gathered)
                )
        sums.append(weight * gathered)
        if len(refs) > 1:
            sums[-1] = sums[-1] + refs[0][: 2 * bands, chunk * lanes : (chunk + 1) * lanes]
    later = jnp.where(lax.axis_index("row") * ratio + fast > lax.axis_index("hist"), 1.0, 0.0)
    extra = sent_ref[taken:, :bands].astype(F32)
    above_log = later * (extra[0:1] + extra[1:2] + extra[2:3])
    above_phase = later * (extra[3:4] + extra[4:5] + extra[5:6])
    if len(refs) > 1:
        above_log = above_log + refs[0][2 * bands : 2 * bands + 1, :bands]
        above_phase = above_phase + refs[0][2 * bands + 1 : 2 * bands + 2, :bands]
    if turn == 0:
        pack_sum(out_ref, bands, sums, (above_log, above_phase))
        return
    for chunk, part in enumerate(sums):
        out_ref[: 2 * bands, chunk * lanes : (chunk + 1) * lanes] = part
    at = lax.broadcasted_iota(jnp.int32, (8, bands), 0)
    out_ref[2 * bands :, :] = jnp.zeros((8, steps * bands), F32)
    out_ref[2 * bands :, :bands] = jnp.where(at == 0, above_log, jnp.where(at == 1, above_phase, 0.0))


def pieces_of(totals):
    shape = (EXTRA, totals[0].shape[1])
    row = lax.broadcasted_iota(jnp.int32, shape, 0)
    extra = jnp.zeros(shape, F32)
    at = 0
    for total in totals:
        for _ in range(3):
            piece = total.astype(BF16).astype(F32)
            extra = jnp.where(row == at, piece, extra)
            total = total - piece
            at += 1
    return extra


def pack_sum(out_ref, bands, chunks, above):
    last = len(chunks) * 2 * bands
    for k, part in enumerate(chunks):
        out_ref[2 * bands * k : 2 * bands * (k + 1), :] = part.astype(BF16)
    out_ref[last:, :] = jnp.zeros((EXTRA, 4 * bands), BF16)
    out_ref[last:, :bands] = pieces_of(above).astype(BF16)


def unpack_sum(own_ref, other_ref, bands):
    last = own_ref.shape[0] - EXTRA
    total = own_ref[...].astype(F32) + other_ref[...].astype(F32)
    chunks = [total[2 * bands * k : 2 * bands * (k + 1)] for k in range(last // (2 * bands))]
    extra = total[last:, :bands]
    return chunks, (extra[0:1] + extra[1:2] + extra[2:3], extra[3:4] + extra[4:5] + extra[5:6])


def narrow_kernel(bands, own_ref, other_ref, out_ref):
    pack_sum(out_ref, bands, *unpack_sum(own_ref, other_ref, bands))


def step_kernel(
    bands, steps, damping_ref, phases_ref, packed_ref, own_ref, other_ref,
    out_ref, square_ref
):
    lanes = 4 * bands
    groups = bands // 4
    chunks, (above_log, above_phase) = unpack_sum(own_ref, other_ref, bands)
    at = lax.broadcasted_iota(jnp.int32, (steps, bands), 0)
    rates = jnp.log(damping_ref[...])
    phases = phases_ref[...]
    summed_log = jnp.broadcast_to(above_log, (steps, bands))
    summed_phase = jnp.broadcast_to(above_phase, (steps, bands))
    for step in range(steps):
        summed_log = summed_log + jnp.where(at <= step, rates[step : step + 1], 0.0)
        summed_phase = summed_phase + jnp.where(at <= step, phases[step : step + 1], 0.0)
    magnitude = jnp.exp(summed_log)
    both = jnp.concatenate(
        [magnitude * jnp.cos(summed_phase), -magnitude * jnp.sin(summed_phase)], axis=1
    )
    wide = lax.broadcasted_iota(jnp.int32, (steps, steps * bands), 1) // bands
    place = lax.broadcasted_iota(jnp.int32, (steps, steps * bands), 0)
    spreading = jnp.where(wide == place, 1.0, 0.0)
    factor = lax.dot_general(
        both, spreading, (((0,), (0,)), ((), ())), precision=HIGHEST, preferred_element_type=F32
    )
    row = packed_ref[...] + jnp.concatenate(chunks, axis=1)
    row_real, row_imag = (row[:bands], row[bands:])
    factor_real, factor_imag = (factor[:bands], factor[bands:])
    stepped = (
        factor_real * row_real - factor_imag * row_imag,
        factor_real * row_imag + factor_imag * row_real,
    )
    squares = jnp.sum(stepped[0] * stepped[0] + stepped[1] * stepped[1], keepdims=True)
    square_ref[...] = jnp.broadcast_to(squares, square_ref.shape)
    out_ref[:bands, :] = stepped[0]
    out_ref[bands:, :] = stepped[1]


def relayout_kernel(bands, steps, stepped_ref, out_ref, work):
    lanes = 4 * bands
    groups = bands // 4
    for part in range(2):
        for chunk in range(steps // 4):
            work[part, chunk] = stepped_ref[
                part * bands : (part + 1) * bands, chunk * lanes : (chunk + 1) * lanes
            ]
    for part in range(2):
        for chunk in range(steps // 4):
            blocks = [work[part, chunk, pl.ds(k, groups, stride=4), :] for k in range(4)]
            for k, block in enumerate(swap_blocks(blocks)):
                first = (chunk * 4 + k) * groups * 2 + part
                out_ref[pl.ds(first, groups, stride=2), :] = block


def call(kernel, shapes, scratch, flops, moved, spaces, *operands):
    return pl.pallas_call(
        kernel,
        out_shape=shapes,
        in_specs=[pl.BlockSpec(memory_space=space) for space in spaces],
        out_specs=[pl.BlockSpec(memory_space=pltpu.VMEM)] * len(shapes),
        scratch_shapes=scratch,
        compiler_params=pltpu.CompilerParams(vmem_limit_bytes=VMEM_LIMIT),
        cost_estimate=pl.CostEstimate(flops=flops, bytes_accessed=moved, transcendentals=0),
    )(*operands)


def shards(
    row_less, row_great, coupling, damping, phases, lesser_hist, advanced_hist, retarded_hist
):
    bands = coupling.shape[0]
    lanes = 4 * bands
    groups = bands // 4
    steps = row_less.shape[1]
    rows = lesser_hist.shape[1]
    hist_count, row_count = (lax.axis_size("hist"), lax.axis_size("row"))
    ratio = hist_count // row_count
    all_steps = steps * hist_count
    weight = float(all_steps * bands) ** (-0.5)
    taken = steps * bands
    sds = jax.ShapeDtypeStruct

    def grouped(x):
        x = x.reshape(2, steps, groups, lanes).transpose(1, 2, 0, 3)
        return x.reshape(steps * groups * 2, lanes)

    retarded = retarded_hist.transpose(0, 2, 1, 3)
    vmem = pltpu.VMEM
    (order,) = call(
        functools.partial(order_kernel, bands, steps, ratio),
        [sds((ratio * taken, bands * WINDOW), BF16)],
        [],
        10**10,
        10**7,
        [],
    )
    send, packed = call(
        functools.partial(energy_kernel, bands, steps),
        [sds((taken + EXTRA, lanes), BF16), sds((2 * bands, taken), F32)],
        [vmem((2, 2, steps // 4 * bands, lanes), F32)],
        10**8,
        10**6,
        [pl.ANY] + [vmem] * 5,
        order,
        grouped(row_less),
        grouped(row_great),
        coupling,
        damping,
        phases,
    )
    arrived = [swap_places(send, turn) for turn in range(ratio)]
    column, give = call(
        functools.partial(column_kernel, bands, steps, rows, weight),
        [sds((groups * rows, lanes), F32), sds((groups * rows + 2 * EXTRA, lanes), BF16)],
        [],
        10**9,
        4 * 10**6,
        [vmem] * 2,
        retarded,
        send,
    )

    def add(own, other, kind):
        (out,) = call(
            add_kernel, [sds(own.shape, kind)], [], 10**10, 10**6, [vmem] * 2, own, other
        )
        return out

    got = crossed(give, "hist", 1)
    summed = sds((steps // 4 * 2 * bands + EXTRA, lanes), BF16)
    histories = [lesser_hist.transpose(0, 2, 1, 3), advanced_hist.transpose(0, 2, 1, 3)]
    (rights,) = call(
        functools.partial(right_kernel, bands, steps, rows, ratio, 0),
        [sds((steps * 2 * bands // 4 * WINDOW, 2 * lanes), BF16)],
        [],
        10**4,
        10**4,
        [vmem] * 2,
        *histories,
    )
    order_first, rights = lax.optimization_barrier((order, rights))
    partial_row = []
    for turn in reversed(range(ratio)):
        operands = [order_first] + histories if turn else [order, rights, rights]
        operands += [arrived[turn], *partial_row]
        partial_row = call(
            functools.partial(row_kernel, bands, steps, rows, weight, ratio, turn),
            [summed if turn == 0 else sds((2 * bands + 8, taken), F32)],
            [],
            10**4,
            10**4,
            [vmem] * len(operands),
            *operands,
        )
    partial_row = partial_row[0]
    bit = 1
    while 2 * bit < row_count:
        (partial_row,) = call(
            functools.partial(narrow_kernel, bands),
            [summed],
            [],
            10**4,
            10**4,
            [vmem] * 2,
            partial_row,
            crossed(partial_row, "row", bit),
        )
        bit *= 2
    other = crossed(partial_row, "row", bit)
    column = add(column, got, BF16)
    got = crossed(column, "hist", hist_count // 2)
    stepped, squares = call(
        functools.partial(step_kernel, bands, steps),
        [sds((2 * bands, taken), F32), sds((8, lanes), F32)],
        [],
        10**10,
        10**6,
        [vmem] * 5,
        damping,
        phases,
        packed,
        partial_row,
        other,
    )
    (stepped,) = call(
        functools.partial(relayout_kernel, bands, steps),
        [sds((steps * groups * 2, lanes), F32)],
        [vmem((2, steps // 4, bands, lanes), F32)],
        10**10,
        10**6,
        [vmem],
        stepped,
    )
    ahead = [hist_count >> k for k in range(1, hist_count.bit_length() - 1)]
    beside = ahead[1:] + [1, None]
    for bit, each in zip([1] + ahead, beside):
        other = crossed(squares, "hist", bit)
        if each:
            column = add(column, got, F32)
            got = crossed(column, "hist", each)
            squares = add(squares, other, F32)
    got, other = lax.optimization_barrier((got, other))
    stepped, column = call(
        functools.partial(final_kernel, float(2 * all_steps * bands * bands)),
        [sds(stepped.shape, F32), sds((2, rows, bands * bands), F32)],
        [],
        10**6,
        10**6,
        [vmem] * 5,
        stepped,
        squares,
        other,
        column,
        got,
    )
    stepped = stepped.reshape(steps, groups, 2, lanes).transpose(2, 0, 1, 3)
    return (stepped.reshape(2, steps, bands * bands), column)


def solution(mesh):
    return jax.shard_map(
        shards,
        mesh=mesh,
        in_specs=(
            P(None, "hist", None),
            P(None, "hist", None),
            P(),
            P("hist", None),
            P("hist", None),
            P(None, "row", "hist", None),
            P(None, "row", "hist", None),
            P(None, "row", "hist", None),
        ),
        out_specs=(P(None, "hist", None), P(None, "row", None)),
        check_vma=False,
    )
```

```python
import functools

import jax
import jax.numpy as jnp
from jax import lax
from jax.experimental import pallas as pl
from jax.experimental.pallas import tpu as pltpu
from jax.sharding import PartitionSpec as P

F32, BF16 = (jnp.float32, jnp.bfloat16)
EXTRA = 16
WINDOW = 16
VMEM_LIMIT = 48 * 1024 * 1024


def swap_places(x, turn):
    hist_count, row_count = (lax.axis_size("hist"), lax.axis_size("row"))
    ratio = hist_count // row_count
    cores = 2 if row_count % 2 == 0 else 1
    span = row_count // cores
    pairs = []
    for slow in range(row_count):
        for fast in range(ratio):
            for row in range(row_count):
                source = (slow * ratio + fast) * row_count + row
                shift = turn + (1 if slow in (0, row_count - 1) else 0)
                goal = row % cores * span + (row // cores + shift) % span
                target = (goal * ratio + (fast + turn) % ratio) * row_count + slow
                pairs.append((source, target))
    return lax.ppermute(x, ("hist", "row"), pairs)


def crossed(x, axis, bit):
    size = lax.axis_size(axis)
    return lax.ppermute(x, axis, [(k, k ^ bit) for k in range(size)])


def lane_block(shape, width):
    return lax.broadcasted_iota(jnp.int32, shape, len(shape) - 1) // width


def swap_blocks(parts):
    width = parts[0].shape[1] // 4
    block = lane_block(parts[0].shape, width)
    parts = list(parts)
    for bit in (2, 1):
        new = list(parts)
        for a in range(4):
            if a & bit == 0:
                low, high = (parts[a], parts[a | bit])
                shift = bit * width
                keep = block & bit == 0
                new[a] = jnp.where(keep, low, pltpu.roll(high, shift, 1))
                new[a | bit] = jnp.where(keep, pltpu.roll(low, 4 * width - shift, 1), high)
        parts = new
    return parts


def split_dot(left, right, dims):
    highs = [x.astype(BF16) for x in (left, right)]
    lows = [(x - high.astype(F32)).astype(BF16) for x, high in zip((left, right), highs)]

    def product(a, b):
        return lax.dot_general(a, b, dims, preferred_element_type=F32)

    return product(highs[0], highs[1]) + (product(highs[0], lows[1]) + product(lows[0], highs[1]))


def energy_kernel(bands, steps, order_ref, less_ref, great_ref, coupling_ref, damping_ref, phases_ref, send_ref, packed_ref, work):
    groups = bands // 4
    chunks = steps // 4
    for which, ref in enumerate((less_ref, great_ref)):
        for part in range(2):
            for chunk in range(chunks):
                blocks = [
                    ref[pl.ds((chunk * 4 + k) * groups * 2 + part, groups, stride=2), :]
                    for k in range(4)
                ]
                for k, block in enumerate(swap_blocks(blocks)):
                    work[which, part, pl.ds(chunk * bands + k, groups, stride=4), :] = block
    less_real, less_imag = (work[0, 0], work[0, 1])
    great_real, great_imag = (work[1, 0], work[1, 1])
    polar = jnp.concatenate(
        [
            -(less_real * great_real + less_imag * great_imag),
            -(less_imag * great_real - less_real * great_imag),
        ],
        axis=0,
    )
    coupling = coupling_ref[...]
    wide = jnp.concatenate([coupling] * 4, axis=1)
    tall = jnp.concatenate([wide] * 4, axis=0)
    at_row = lax.broadcasted_iota(jnp.int32, tall.shape, 0) // bands
    blocked = jnp.where(at_row == lane_block(tall.shape, bands), tall, 0.0)
    half = split_dot(polar, blocked, (((1,), (1,)), ((), ())))
    rows = chunks * bands
    both = jnp.concatenate([half[:rows], half[rows:]], axis=1)
    screens = []
    for chunk in range(chunks):
        part = both[chunk * bands : (chunk + 1) * bands]
        screens.append(split_dot(coupling, part, (((1,), (0,)), ((), ()))))
    screen = jnp.concatenate(screens, axis=0)
    lanes = 4 * bands
    screen_real, screen_imag = (screen[:, :lanes], screen[:, lanes:])
    sigma_real = less_real * screen_real - less_imag * screen_imag
    sigma_imag = less_real * screen_imag + less_imag * screen_real
    wide_real = great_real * screen_real + great_imag * screen_imag
    wide_imag = great_imag * screen_real - great_real * screen_imag
    outs = (wide_real - sigma_real, wide_imag - sigma_imag, sigma_real, sigma_imag)
    for chunk in range(chunks):
        at = slice(chunk * bands, (chunk + 1) * bands)
        to = slice(chunk * lanes, (chunk + 1) * lanes)
        for k, out in enumerate(outs):
            first = (chunk * 4 + k) * bands
            send_ref[first : first + bands, :] = out[at].astype(BF16)
        packed_ref[:bands, to] = less_real[at]
        packed_ref[bands:, to] = less_imag[at]
    log_total = jnp.sum(jnp.log(damping_ref[...]), axis=0, keepdims=True)
    phase_total = jnp.sum(phases_ref[...], axis=0, keepdims=True)
    last = steps * bands
    send_ref[last:, :] = jnp.zeros((EXTRA, lanes), BF16)
    send_ref[last:, :bands] = pieces_of((log_total, phase_total)).astype(BF16)


def order_kernel(bands, steps, ratio, order_ref):
    groups = bands // 4
    taken = steps * bands
    source = lax.broadcasted_iota(jnp.int32, (taken, 1), 0)
    band = source % bands
    target = (band % 4) * (groups * WINDOW) + (band // 4) * WINDOW + source // bands
    column = lax.broadcasted_iota(jnp.int32, (taken, order_ref.shape[1]), 1)
    for turn in range(ratio):
        fast = (lax.axis_index("hist") + ratio - turn) % ratio
        hit = column == target + fast * steps % 8
        order_ref[turn * taken : (turn + 1) * taken, :] = jnp.where(hit, 1.0, 0.0).astype(BF16)


def column_kernel(bands, steps, rows, weight, retarded_ref, send_ref, keep_ref, give_ref):
    lanes = 4 * bands
    groups = bands // 4
    hist_start, row_start = (lax.axis_index("hist") * steps, lax.axis_index("row") * rows)
    block = lane_block((bands, lanes), bands)
    later = row_start + lax.broadcasted_iota(jnp.int32, (rows, groups * lanes), 0)
    total = None
    for chunk in range(steps // 4):
        turned = []
        for part in range(2):
            first = (chunk * 4 + 2 + part) * bands
            own = send_ref[first : first + bands, :].astype(F32)
            turned.append([own] + [pltpu.roll(own, d * bands, 1) for d in range(1, 4)])
        for k in range(4):
            step = chunk * 4 + k
            real, imag = [
                jnp.concatenate(
                    [jnp.where(block == b, turned[part][(b - k) % 4], 0.0) for b in range(4)],
                    axis=0,
                )
                for part in range(2)
            ]
            weights = jnp.concatenate(
                [
                    jnp.concatenate([real, imag], axis=1),
                    jnp.concatenate([-imag, real], axis=1),
                ],
                axis=0,
            ).astype(BF16)
            causal = hist_start + step <= later
            halves = []
            for part in range(2):
                whole = jnp.where(causal, retarded_ref[part, step].astype(F32), 0.0)
                halves.append(
                    jnp.concatenate(
                        [whole[:, g * lanes : (g + 1) * lanes] for g in range(groups)], axis=0
                    ).astype(BF16)
                )
            term = lax.dot_general(
                jnp.concatenate(halves, axis=1),
                weights,
                (((1,), (1,)), ((), ())),
                preferred_element_type=F32,
            )
            total = term if total is None else total + term
    low = lax.axis_index("hist") % 2 == 0
    give_ref[groups * rows :, :] = jnp.zeros((give_ref.shape[0] - groups * rows, lanes), BF16)
    for g in range(groups // 2):
        for part in range(2):
            halves = [
                -weight * total[k * rows : (k + 1) * rows, part * lanes : (part + 1) * lanes]
                for k in (g, g + groups // 2)
            ]
            to = slice((2 * g + part) * rows, (2 * g + part + 1) * rows)
            keep_ref[to, :] = jnp.where(low, halves[0], halves[1])
            give_ref[to, :] = jnp.where(low, halves[1], halves[0]).astype(BF16)


def add_kernel(own_ref, other_ref, out_ref):
    total = own_ref[...].astype(F32) + other_ref[: own_ref.shape[0], :].astype(F32)
    out_ref[...] = total.astype(out_ref.dtype)


def final_kernel(count, stepped_ref, own_ref, other_ref, sum_ref, more_ref, row_ref, column_ref):
    squares = (own_ref[...] + other_ref[...])[0:1]
    row_ref[...] = stepped_ref[...] / jnp.sqrt(squares / count + 1e-06)
    low = lax.axis_index("hist") % 2 == 0
    half, back = (sum_ref[...], more_ref[...])
    column = jnp.concatenate([jnp.where(low, half, back), jnp.where(low, back, half)], axis=0)
    rows, lanes = (column_ref.shape[1], column.shape[1])
    for part in range(2):
        for g in range(column_ref.shape[2] // lanes):
            at = (2 * g + part) * rows
            column_ref[part, :, g * lanes : (g + 1) * lanes] = column[at : at + rows]


def right_operand(bands, steps, rows, ratio, turn, lesser_ref, advanced_ref):
    lanes = 4 * bands
    groups = bands // 4
    fast = (lax.axis_index("hist") + ratio - turn) % ratio
    starts = [f * steps // 8 * 8 for f in range(ratio)]
    start = fast * steps // 8 * 8
    earlier = lax.axis_index("row") * rows + start
    earlier = earlier + lax.broadcasted_iota(jnp.int32, (WINDOW, groups * lanes), 0)
    hist_start = lax.axis_index("hist") * steps

    def right(which, step):
        ref = (lesser_ref, advanced_ref)[which]
        pieces = []
        for part in range(2):
            whole = ref[part, step].astype(F32)
            window = whole[:WINDOW]
            for f in range(1, ratio):
                window = jnp.where(fast == f, whole[starts[f] : starts[f] + WINDOW], window)
            if which == 1:
                window = jnp.where(earlier <= hist_start + step, window, 0.0)
            pieces += [window[:, g * lanes : (g + 1) * lanes] for g in range(groups)]
        return jnp.concatenate(pieces, axis=0).astype(BF16)

    return right


def right_kernel(bands, steps, rows, ratio, turn, lesser_ref, advanced_ref, out_ref):
    right = right_operand(bands, steps, rows, ratio, turn, lesser_ref, advanced_ref)
    depth = 2 * bands // 4 * WINDOW
    for which in range(2):
        for pair in range(steps // 2):
            at = (which * steps // 2 + pair) * depth
            both = [right(which, 2 * pair), right(which, 2 * pair + 1)]
            out_ref[at : at + depth, :] = jnp.concatenate(both, axis=1)


def row_kernel(bands, steps, rows, weight, ratio, turn, order_ref, lesser_ref, advanced_ref, sent_ref, *refs):
    out_ref = refs[-1]
    lanes = 4 * bands
    groups = bands // 4
    depth = groups * WINDOW
    taken = steps * bands
    fast = (lax.axis_index("hist") + ratio - turn) % ratio
    sigma = jnp.concatenate([sent_ref[c * lanes : (c + 1) * lanes, :] for c in range(steps // 4)], axis=1)
    ordered = jnp.dot(
        sigma,
        order_ref[turn * taken : (turn + 1) * taken, :],
        preferred_element_type=F32,
    )
    lefts = []
    for which in range(2):
        real = ordered[2 * which * bands : (2 * which + 1) * bands]
        imag = ordered[(2 * which + 1) * bands : (2 * which + 2) * bands]
        both = []
        for k in range(4):
            at = slice(k * depth, (k + 1) * depth)
            both.append(jnp.concatenate([real[:, at], -imag[:, at]], axis=1))
            both.append(jnp.concatenate([imag[:, at], real[:, at]], axis=1))
        lefts.append(jnp.concatenate(both, axis=0).astype(BF16))
    built = len(lesser_ref.shape) == 2
    if not built:
        right = right_operand(bands, steps, rows, ratio, turn, lesser_ref, advanced_ref)

    block = lane_block((2 * bands, lanes), bands)
    sums = []
    for chunk in range(steps // 4):
        gathered = None
        for pair in range(2):
            first = chunk * 4 + pair * 2
            total = None
            for which in range(2):
                if built:
                    at = (which * steps // 2 + first // 2) * 2 * depth
                    rights = lesser_ref[at : at + 2 * depth, :]
                else:
                    rights = jnp.concatenate([right(which, first), right(which, first + 1)], axis=1)
                term = jnp.dot(lefts[which], rights, preferred_element_type=F32)
                total = term if total is None else total + term
            for k in range(2):
                own = total[:, k * lanes : (k + 1) * lanes]
                picked = own[: 2 * bands]
                for b in range(1, 4):
                    picked = jnp.where(block == b, own[2 * bands * b : 2 * bands * (b + 1)], picked)
                picked = picked + pltpu.roll(picked, 2 * bands, 1)
                picked = picked + pltpu.roll(picked, bands, 1)
                gathered = (
                    picked if gathered is None else jnp.where(block == 2 * pair + k, picked, gathered)
                )
        sums.append(weight * gathered)
        if len(refs) > 1:
            sums[-1] = sums[-1] + refs[0][: 2 * bands, chunk * lanes : (chunk + 1) * lanes]
    later = jnp.where(lax.axis_index("row") * ratio + fast > lax.axis_index("hist"), 1.0, 0.0)
    extra = sent_ref[taken:, :bands].astype(F32)
    above_log = later * (extra[0:1] + extra[1:2] + extra[2:3])
    above_phase = later * (extra[3:4] + extra[4:5] + extra[5:6])
    if len(refs) > 1:
        above_log = above_log + refs[0][2 * bands : 2 * bands + 1, :bands]
        above_phase = above_phase + refs[0][2 * bands + 1 : 2 * bands + 2, :bands]
    if turn == 0:
        pack_sum(out_ref, bands, sums, (above_log, above_phase))
        return
    for chunk, part in enumerate(sums):
        out_ref[: 2 * bands, chunk * lanes : (chunk + 1) * lanes] = part
    at = lax.broadcasted_iota(jnp.int32, (8, bands), 0)
    out_ref[2 * bands :, :] = jnp.zeros((8, steps * bands), F32)
    out_ref[2 * bands :, :bands] = jnp.where(at == 0, above_log, jnp.where(at == 1, above_phase, 0.0))


def pieces_of(totals):
    shape = (EXTRA, totals[0].shape[1])
    row = lax.broadcasted_iota(jnp.int32, shape, 0)
    extra = jnp.zeros(shape, F32)
    at = 0
    for total in totals:
        for _ in range(3):
            piece = total.astype(BF16).astype(F32)
            extra = jnp.where(row == at, piece, extra)
            total = total - piece
            at += 1
    return extra


def pack_sum(out_ref, bands, chunks, above):
    last = len(chunks) * 2 * bands
    for k, part in enumerate(chunks):
        out_ref[2 * bands * k : 2 * bands * (k + 1), :] = part.astype(BF16)
    out_ref[last:, :] = jnp.zeros((EXTRA, 4 * bands), BF16)
    out_ref[last:, :bands] = pieces_of(above).astype(BF16)


def unpack_sum(own_ref, other_ref, bands):
    last = own_ref.shape[0] - EXTRA
    total = own_ref[...].astype(F32) + other_ref[...].astype(F32)
    chunks = [total[2 * bands * k : 2 * bands * (k + 1)] for k in range(last // (2 * bands))]
    extra = total[last:, :bands]
    return chunks, (extra[0:1] + extra[1:2] + extra[2:3], extra[3:4] + extra[4:5] + extra[5:6])


def narrow_kernel(bands, own_ref, other_ref, out_ref):
    pack_sum(out_ref, bands, *unpack_sum(own_ref, other_ref, bands))


def step_kernel(
    bands, steps, damping_ref, phases_ref, packed_ref, own_ref, other_ref,
    out_ref, square_ref
):
    lanes = 4 * bands
    groups = bands // 4
    chunks, (above_log, above_phase) = unpack_sum(own_ref, other_ref, bands)
    at = lax.broadcasted_iota(jnp.int32, (steps, bands), 0)
    rates = jnp.log(damping_ref[...])
    phases = phases_ref[...]
    summed_log = jnp.broadcast_to(above_log, (steps, bands))
    summed_phase = jnp.broadcast_to(above_phase, (steps, bands))
    for step in range(steps):
        summed_log = summed_log + jnp.where(at <= step, rates[step : step + 1], 0.0)
        summed_phase = summed_phase + jnp.where(at <= step, phases[step : step + 1], 0.0)
    magnitude = jnp.exp(summed_log)
    both = jnp.concatenate(
        [magnitude * jnp.cos(summed_phase), -magnitude * jnp.sin(summed_phase)], axis=1
    )
    wide = lax.broadcasted_iota(jnp.int32, (steps, steps * bands), 1) // bands
    place = lax.broadcasted_iota(jnp.int32, (steps, steps * bands), 0)
    spreading = jnp.where(wide == place, 1.0, 0.0).astype(BF16)
    factor = jnp.zeros((2 * bands, steps * bands), F32)
    for _ in range(3):
        piece = both.astype(BF16)
        both = both - piece.astype(F32)
        factor = factor + lax.dot_general(
            piece, spreading, (((0,), (0,)), ((), ())), preferred_element_type=F32
        )
    row = packed_ref[...] + jnp.concatenate(chunks, axis=1)
    row_real, row_imag = (row[:bands], row[bands:])
    factor_real, factor_imag = (factor[:bands], factor[bands:])
    stepped = (
        factor_real * row_real - factor_imag * row_imag,
        factor_real * row_imag + factor_imag * row_real,
    )
    squares = jnp.sum(stepped[0] * stepped[0] + stepped[1] * stepped[1], keepdims=True)
    square_ref[...] = jnp.broadcast_to(squares, square_ref.shape)
    out_ref[:bands, :] = stepped[0]
    out_ref[bands:, :] = stepped[1]


def relayout_kernel(bands, steps, stepped_ref, out_ref, work):
    lanes = 4 * bands
    groups = bands // 4
    for part in range(2):
        for chunk in range(steps // 4):
            work[part, chunk] = stepped_ref[
                part * bands : (part + 1) * bands, chunk * lanes : (chunk + 1) * lanes
            ]
    for part in range(2):
        for chunk in range(steps // 4):
            blocks = [work[part, chunk, pl.ds(k, groups, stride=4), :] for k in range(4)]
            for k, block in enumerate(swap_blocks(blocks)):
                first = (chunk * 4 + k) * groups * 2 + part
                out_ref[pl.ds(first, groups, stride=2), :] = block


def call(kernel, shapes, scratch, flops, moved, spaces, *operands):
    return pl.pallas_call(
        kernel,
        out_shape=shapes,
        in_specs=[pl.BlockSpec(memory_space=space) for space in spaces],
        out_specs=[pl.BlockSpec(memory_space=pltpu.VMEM)] * len(shapes),
        scratch_shapes=scratch,
        compiler_params=pltpu.CompilerParams(vmem_limit_bytes=VMEM_LIMIT),
        cost_estimate=pl.CostEstimate(flops=flops, bytes_accessed=moved, transcendentals=0),
    )(*operands)


def shards(
    row_less, row_great, coupling, damping, phases, lesser_hist, advanced_hist, retarded_hist
):
    bands = coupling.shape[0]
    lanes = 4 * bands
    groups = bands // 4
    steps = row_less.shape[1]
    rows = lesser_hist.shape[1]
    hist_count, row_count = (lax.axis_size("hist"), lax.axis_size("row"))
    ratio = hist_count // row_count
    all_steps = steps * hist_count
    weight = float(all_steps * bands) ** (-0.5)
    taken = steps * bands
    sds = jax.ShapeDtypeStruct

    def grouped(x):
        x = x.reshape(2, steps, groups, lanes).transpose(1, 2, 0, 3)
        return x.reshape(steps * groups * 2, lanes)

    retarded = retarded_hist.transpose(0, 2, 1, 3)
    vmem = pltpu.VMEM
    (order,) = call(
        functools.partial(order_kernel, bands, steps, ratio),
        [sds((ratio * taken, bands * WINDOW), BF16)],
        [],
        10**10,
        10**7,
        [],
    )
    send, packed = call(
        functools.partial(energy_kernel, bands, steps),
        [sds((taken + EXTRA, lanes), BF16), sds((2 * bands, taken), F32)],
        [vmem((2, 2, steps // 4 * bands, lanes), F32)],
        10**8,
        10**6,
        [pl.ANY] + [vmem] * 5,
        order,
        grouped(row_less),
        grouped(row_great),
        coupling,
        damping,
        phases,
    )
    arrived = [swap_places(send, turn) for turn in range(ratio)]
    column, give = call(
        functools.partial(column_kernel, bands, steps, rows, weight),
        [sds((groups * rows, lanes), F32), sds((groups * rows + 2 * EXTRA, lanes), BF16)],
        [],
        10**9,
        4 * 10**6,
        [vmem] * 2,
        retarded,
        send,
    )

    def add(own, other, kind):
        (out,) = call(
            add_kernel, [sds(own.shape, kind)], [], 10**10, 10**6, [vmem] * 2, own, other
        )
        return out

    got = crossed(give, "hist", 1)
    summed = sds((steps // 4 * 2 * bands + EXTRA, lanes), BF16)
    histories = [lesser_hist.transpose(0, 2, 1, 3), advanced_hist.transpose(0, 2, 1, 3)]
    (rights,) = call(
        functools.partial(right_kernel, bands, steps, rows, ratio, 0),
        [sds((steps * 2 * bands // 4 * WINDOW, 2 * lanes), BF16)],
        [],
        10**4,
        10**4,
        [vmem] * 2,
        *histories,
    )
    order_first, rights = lax.optimization_barrier((order, rights))
    partial_row = []
    for turn in reversed(range(ratio)):
        operands = [order_first] + histories if turn else [order, rights, rights]
        operands += [arrived[turn], *partial_row]
        partial_row = call(
            functools.partial(row_kernel, bands, steps, rows, weight, ratio, turn),
            [summed if turn == 0 else sds((2 * bands + 8, taken), F32)],
            [],
            10**4,
            10**4,
            [vmem] * len(operands),
            *operands,
        )
    partial_row = partial_row[0]
    bit = 1
    while 2 * bit < row_count:
        (partial_row,) = call(
            functools.partial(narrow_kernel, bands),
            [summed],
            [],
            10**4,
            10**4,
            [vmem] * 2,
            partial_row,
            crossed(partial_row, "row", bit),
        )
        bit *= 2
    other = crossed(partial_row, "row", bit)
    column = add(column, got, BF16)
    got = crossed(column, "hist", hist_count // 2)
    stepped, squares = call(
        functools.partial(step_kernel, bands, steps),
        [sds((2 * bands, taken), F32), sds((1, lanes), F32)],
        [],
        10**10,
        10**6,
        [vmem] * 5,
        damping,
        phases,
        packed,
        partial_row,
        other,
    )
    (stepped,) = call(
        functools.partial(relayout_kernel, bands, steps),
        [sds((steps * groups * 2, lanes), F32)],
        [vmem((2, steps // 4, bands, lanes), F32)],
        10**10,
        10**6,
        [vmem],
        stepped,
    )
    ahead = [hist_count >> k for k in range(1, hist_count.bit_length() - 1)]
    beside = ahead[1:] + [1, None]
    for bit, each in zip([1] + ahead, beside):
        other = crossed(squares, "hist", bit)
        if each:
            column = add(column, got, F32)
            got = crossed(column, "hist", each)
            squares = add(squares, other, F32)
    got, other = lax.optimization_barrier((got, other))
    stepped, column = call(
        functools.partial(final_kernel, float(2 * all_steps * bands * bands)),
        [sds(stepped.shape, F32), sds((2, rows, bands * bands), F32)],
        [],
        10**6,
        10**6,
        [vmem] * 5,
        stepped,
        squares,
        other,
        column,
        got,
    )
    stepped = stepped.reshape(steps, groups, 2, lanes).transpose(2, 0, 1, 3)
    return (stepped.reshape(2, steps, bands * bands), column)


def solution(mesh):
    return jax.shard_map(
        shards,
        mesh=mesh,
        in_specs=(
            P(None, "hist", None),
            P(None, "hist", None),
            P(),
            P("hist", None),
            P("hist", None),
            P(None, "row", "hist", None),
            P(None, "row", "hist", None),
            P(None, "row", "hist", None),
        ),
        out_specs=(P(None, "hist", None), P(None, "row", None)),
        check_vma=False,
    )
```

```python
import functools

import jax
import jax.numpy as jnp
from jax import lax
from jax.experimental import pallas as pl
from jax.experimental.pallas import tpu as pltpu
from jax.sharding import PartitionSpec as P

F32, BF16 = (jnp.float32, jnp.bfloat16)
EXTRA = 16
WINDOW = 16
VMEM_LIMIT = 48 * 1024 * 1024


def swap_places(x, turn):
    hist_count, row_count = (lax.axis_size("hist"), lax.axis_size("row"))
    ratio = hist_count // row_count
    cores = 2 if row_count % 2 == 0 else 1
    span = row_count // cores
    pairs = []
    for slow in range(row_count):
        for fast in range(ratio):
            for row in range(row_count):
                source = (slow * ratio + fast) * row_count + row
                shift = turn + (1 if slow in (0, row_count - 1) else 0)
                goal = row % cores * span + (row // cores + shift) % span
                target = (goal * ratio + (fast + turn) % ratio) * row_count + slow
                pairs.append((source, target))
    return lax.ppermute(x, ("hist", "row"), pairs)


def crossed(x, axis, bit):
    size = lax.axis_size(axis)
    return lax.ppermute(x, axis, [(k, k ^ bit) for k in range(size)])


def lane_block(shape, width):
    return lax.broadcasted_iota(jnp.int32, shape, len(shape) - 1) // width


def swap_blocks(parts):
    width = parts[0].shape[1] // 4
    block = lane_block(parts[0].shape, width)
    parts = list(parts)
    for bit in (2, 1):
        new = list(parts)
        for a in range(4):
            if a & bit == 0:
                low, high = (parts[a], parts[a | bit])
                shift = bit * width
                keep = block & bit == 0
                new[a] = jnp.where(keep, low, pltpu.roll(high, shift, 1))
                new[a | bit] = jnp.where(keep, pltpu.roll(low, 4 * width - shift, 1), high)
        parts = new
    return parts


def split_dot(left, right, dims):
    highs = [x.astype(BF16) for x in (left, right)]
    lows = [(x - high.astype(F32)).astype(BF16) for x, high in zip((left, right), highs)]

    def product(a, b):
        return lax.dot_general(a, b, dims, preferred_element_type=F32)

    return product(highs[0], highs[1]) + (product(highs[0], lows[1]) + product(lows[0], highs[1]))


def energy_kernel(bands, steps, order_ref, less_ref, great_ref, coupling_ref, damping_ref, phases_ref, send_ref, packed_ref, mixed, work):
    groups = bands // 4
    chunks = steps // 4
    for which, ref in enumerate((less_ref, great_ref)):
        mixed[which, : ref.shape[0], :] = ref[...]
        for part in range(2):
            for chunk in range(chunks):
                blocks = [
                    mixed[which, pl.ds((chunk * 4 + k) * groups * 2 + part, groups, stride=2), :]
                    for k in range(4)
                ]
                for k, block in enumerate(swap_blocks(blocks)):
                    work[which, part, pl.ds(chunk * bands + k, groups, stride=4), :] = block
    rows = chunks * bands
    less_real, less_imag = (work[0, 0, :rows], work[0, 1, :rows])
    great_real, great_imag = (work[1, 0, :rows], work[1, 1, :rows])
    polar = jnp.concatenate(
        [
            -(less_real * great_real + less_imag * great_imag),
            -(less_imag * great_real - less_real * great_imag),
        ],
        axis=0,
    )
    coupling = coupling_ref[...]
    wide = jnp.concatenate([coupling] * 4, axis=1)
    tall = jnp.concatenate([wide] * 4, axis=0)
    at_row = lax.broadcasted_iota(jnp.int32, tall.shape, 0) // bands
    blocked = jnp.where(at_row == lane_block(tall.shape, bands), tall, 0.0)
    half = split_dot(polar, blocked, (((1,), (1,)), ((), ())))
    rows = chunks * bands
    both = jnp.concatenate([half[:rows], half[rows:]], axis=1)
    screens = []
    for chunk in range(chunks):
        part = both[chunk * bands : (chunk + 1) * bands]
        screens.append(split_dot(coupling, part, (((1,), (0,)), ((), ()))))
    screen = jnp.concatenate(screens, axis=0)
    lanes = 4 * bands
    screen_real, screen_imag = (screen[:, :lanes], screen[:, lanes:])
    sigma_real = less_real * screen_real - less_imag * screen_imag
    sigma_imag = less_real * screen_imag + less_imag * screen_real
    wide_real = great_real * screen_real + great_imag * screen_imag
    wide_imag = great_imag * screen_real - great_real * screen_imag
    outs = (wide_real - sigma_real, wide_imag - sigma_imag, sigma_real, sigma_imag)
    for chunk in range(chunks):
        at = slice(chunk * bands, (chunk + 1) * bands)
        to = slice(chunk * lanes, (chunk + 1) * lanes)
        for k, out in enumerate(outs):
            first = (chunk * 4 + k) * bands
            send_ref[first : first + bands, :] = out[at].astype(BF16)
        packed_ref[:bands, to] = less_real[at]
        packed_ref[bands:, to] = less_imag[at]
    log_total = jnp.sum(jnp.log(damping_ref[...]), axis=0, keepdims=True)
    phase_total = jnp.sum(phases_ref[...], axis=0, keepdims=True)
    last = steps * bands
    send_ref[last:, :] = jnp.zeros((EXTRA, lanes), BF16)
    send_ref[last:, :bands] = pieces_of((log_total, phase_total)).astype(BF16)


def order_kernel(bands, steps, ratio, order_ref):
    groups = bands // 4
    taken = steps * bands
    source = lax.broadcasted_iota(jnp.int32, (taken, 1), 0)
    band = source % bands
    target = (band % 4) * (groups * WINDOW) + (band // 4) * WINDOW + source // bands
    column = lax.broadcasted_iota(jnp.int32, (taken, order_ref.shape[1]), 1)
    for turn in range(ratio):
        fast = (lax.axis_index("hist") + ratio - turn) % ratio
        hit = column == target + fast * steps % 8
        order_ref[turn * taken : (turn + 1) * taken, :] = jnp.where(hit, 1.0, 0.0).astype(BF16)


def column_kernel(bands, steps, rows, weight, retarded_ref, send_ref, keep_ref, give_ref):
    lanes = 4 * bands
    groups = bands // 4
    hist_start, row_start = (lax.axis_index("hist") * steps, lax.axis_index("row") * rows)
    block = lane_block((bands, lanes), bands)
    later = row_start + lax.broadcasted_iota(jnp.int32, (rows, groups * lanes), 0)
    total = None
    for chunk in range(steps // 4):
        turned = []
        for part in range(2):
            first = (chunk * 4 + 2 + part) * bands
            own = send_ref[first : first + bands, :].astype(F32)
            turned.append([own] + [pltpu.roll(own, d * bands, 1) for d in range(1, 4)])
        for k in range(4):
            step = chunk * 4 + k
            real, imag = [
                jnp.concatenate(
                    [jnp.where(block == b, turned[part][(b - k) % 4], 0.0) for b in range(4)],
                    axis=0,
                )
                for part in range(2)
            ]
            weights = jnp.concatenate(
                [
                    jnp.concatenate([real, imag], axis=1),
                    jnp.concatenate([-imag, real], axis=1),
                ],
                axis=0,
            ).astype(BF16)
            causal = hist_start + step <= later
            halves = []
            for part in range(2):
                whole = jnp.where(causal, retarded_ref[part, step].astype(F32), 0.0)
                halves.append(
                    jnp.concatenate(
                        [whole[:, g * lanes : (g + 1) * lanes] for g in range(groups)], axis=0
                    ).astype(BF16)
                )
            term = lax.dot_general(
                jnp.concatenate(halves, axis=1),
                weights,
                (((1,), (1,)), ((), ())),
                preferred_element_type=F32,
            )
            total = term if total is None else total + term
    low = lax.axis_index("hist") % 2 == 0
    give_ref[groups * rows :, :] = jnp.zeros((give_ref.shape[0] - groups * rows, lanes), BF16)
    for g in range(groups // 2):
        for part in range(2):
            halves = [
                -weight * total[k * rows : (k + 1) * rows, part * lanes : (part + 1) * lanes]
                for k in (g, g + groups // 2)
            ]
            to = slice((2 * g + part) * rows, (2 * g + part + 1) * rows)
            keep_ref[to, :] = jnp.where(low, halves[0], halves[1])
            give_ref[to, :] = jnp.where(low, halves[1], halves[0]).astype(BF16)


def add_kernel(own_ref, other_ref, out_ref):
    total = own_ref[...].astype(F32) + other_ref[: own_ref.shape[0], :].astype(F32)
    out_ref[...] = total.astype(out_ref.dtype)


def final_kernel(count, stepped_ref, own_ref, other_ref, sum_ref, more_ref, row_ref, column_ref):
    squares = (own_ref[...] + other_ref[...])[0:1]
    row_ref[...] = stepped_ref[...] / jnp.sqrt(squares / count + 1e-06)
    low = lax.axis_index("hist") % 2 == 0
    half, back = (sum_ref[...], more_ref[...])
    column = jnp.concatenate([jnp.where(low, half, back), jnp.where(low, back, half)], axis=0)
    rows, lanes = (column_ref.shape[1], column.shape[1])
    for part in range(2):
        for g in range(column_ref.shape[2] // lanes):
            at = (2 * g + part) * rows
            column_ref[part, :, g * lanes : (g + 1) * lanes] = column[at : at + rows]


def right_operand(bands, steps, rows, ratio, turn, lesser_ref, advanced_ref):
    lanes = 4 * bands
    groups = bands // 4
    fast = (lax.axis_index("hist") + ratio - turn) % ratio
    starts = [f * steps // 8 * 8 for f in range(ratio)]
    start = fast * steps // 8 * 8
    earlier = lax.axis_index("row") * rows + start
    earlier = earlier + lax.broadcasted_iota(jnp.int32, (WINDOW, groups * lanes), 0)
    hist_start = lax.axis_index("hist") * steps

    def right(which, step):
        ref = (lesser_ref, advanced_ref)[which]
        pieces = []
        for part in range(2):
            whole = ref[part, step].astype(F32)
            window = whole[:WINDOW]
            for f in range(1, ratio):
                window = jnp.where(fast == f, whole[starts[f] : starts[f] + WINDOW], window)
            if which == 1:
                window = jnp.where(earlier <= hist_start + step, window, 0.0)
            pieces += [window[:, g * lanes : (g + 1) * lanes] for g in range(groups)]
        return jnp.concatenate(pieces, axis=0).astype(BF16)

    return right


def right_kernel(bands, steps, rows, ratio, turn, lesser_ref, advanced_ref, out_ref):
    right = right_operand(bands, steps, rows, ratio, turn, lesser_ref, advanced_ref)
    depth = 2 * bands // 4 * WINDOW
    for which in range(2):
        for pair in range(steps // 2):
            at = (which * steps // 2 + pair) * depth
            both = [right(which, 2 * pair), right(which, 2 * pair + 1)]
            out_ref[at : at + depth, :] = jnp.concatenate(both, axis=1)


def row_kernel(bands, steps, rows, weight, ratio, turn, order_ref, lesser_ref, advanced_ref, sent_ref, *refs):
    out_ref = refs[-1]
    lanes = 4 * bands
    groups = bands // 4
    depth = groups * WINDOW
    taken = steps * bands
    fast = (lax.axis_index("hist") + ratio - turn) % ratio
    sigma = jnp.concatenate([sent_ref[c * lanes : (c + 1) * lanes, :] for c in range(steps // 4)], axis=1)
    ordered = jnp.dot(
        sigma,
        order_ref[turn * taken : (turn + 1) * taken, :],
        preferred_element_type=F32,
    )
    lefts = []
    for which in range(2):
        real = ordered[2 * which * bands : (2 * which + 1) * bands]
        imag = ordered[(2 * which + 1) * bands : (2 * which + 2) * bands]
        both = []
        for k in range(4):
            at = slice(k * depth, (k + 1) * depth)
            both.append(jnp.concatenate([real[:, at], -imag[:, at]], axis=1))
            both.append(jnp.concatenate([imag[:, at], real[:, at]], axis=1))
        lefts.append(jnp.concatenate(both, axis=0).astype(BF16))
    built = len(lesser_ref.shape) == 2
    if not built:
        right = right_operand(bands, steps, rows, ratio, turn, lesser_ref, advanced_ref)

    block = lane_block((2 * bands, lanes), bands)
    sums = []
    for chunk in range(steps // 4):
        gathered = None
        for pair in range(2):
            first = chunk * 4 + pair * 2
            total = None
            for which in range(2):
                if built:
                    at = (which * steps // 2 + first // 2) * 2 * depth
                    rights = lesser_ref[at : at + 2 * depth, :]
                else:
                    rights = jnp.concatenate([right(which, first), right(which, first + 1)], axis=1)
                term = jnp.dot(lefts[which], rights, preferred_element_type=F32)
                total = term if total is None else total + term
            for k in range(2):
                own = total[:, k * lanes : (k + 1) * lanes]
                picked = own[: 2 * bands]
                for b in range(1, 4):
                    picked = jnp.where(block == b, own[2 * bands * b : 2 * bands * (b + 1)], picked)
                picked = picked + pltpu.roll(picked, 2 * bands, 1)
                picked = picked + pltpu.roll(picked, bands, 1)
                gathered = (
                    picked if gathered is None else jnp.where(block == 2 * pair + k, picked, gathered)
                )
        sums.append(weight * gathered)
        if len(refs) > 1:
            sums[-1] = sums[-1] + refs[0][: 2 * bands, chunk * lanes : (chunk + 1) * lanes]
    later = jnp.where(lax.axis_index("row") * ratio + fast > lax.axis_index("hist"), 1.0, 0.0)
    extra = sent_ref[taken:, :bands].astype(F32)
    above_log = later * (extra[0:1] + extra[1:2] + extra[2:3])
    above_phase = later * (extra[3:4] + extra[4:5] + extra[5:6])
    if len(refs) > 1:
        above_log = above_log + refs[0][2 * bands : 2 * bands + 1, :bands]
        above_phase = above_phase + refs[0][2 * bands + 1 : 2 * bands + 2, :bands]
    if turn == 0:
        pack_sum(out_ref, bands, sums, (above_log, above_phase))
        return
    for chunk, part in enumerate(sums):
        out_ref[: 2 * bands, chunk * lanes : (chunk + 1) * lanes] = part
    at = lax.broadcasted_iota(jnp.int32, (8, bands), 0)
    out_ref[2 * bands :, :] = jnp.zeros((8, steps * bands), F32)
    out_ref[2 * bands :, :bands] = jnp.where(at == 0, above_log, jnp.where(at == 1, above_phase, 0.0))


def pieces_of(totals):
    shape = (EXTRA, totals[0].shape[1])
    row = lax.broadcasted_iota(jnp.int32, shape, 0)
    extra = jnp.zeros(shape, F32)
    at = 0
    for total in totals:
        for _ in range(3):
            piece = total.astype(BF16).astype(F32)
            extra = jnp.where(row == at, piece, extra)
            total = total - piece
            at += 1
    return extra


def pack_sum(out_ref, bands, chunks, above):
    last = len(chunks) * 2 * bands
    for k, part in enumerate(chunks):
        out_ref[2 * bands * k : 2 * bands * (k + 1), :] = part.astype(BF16)
    out_ref[last:, :] = jnp.zeros((EXTRA, 4 * bands), BF16)
    out_ref[last:, :bands] = pieces_of(above).astype(BF16)


def unpack_sum(own_ref, other_ref, bands):
    last = own_ref.shape[0] - EXTRA
    total = own_ref[...].astype(F32) + other_ref[...].astype(F32)
    chunks = [total[2 * bands * k : 2 * bands * (k + 1)] for k in range(last // (2 * bands))]
    extra = total[last:, :bands]
    return chunks, (extra[0:1] + extra[1:2] + extra[2:3], extra[3:4] + extra[4:5] + extra[5:6])


def narrow_kernel(bands, own_ref, other_ref, out_ref):
    pack_sum(out_ref, bands, *unpack_sum(own_ref, other_ref, bands))


def step_kernel(
    bands, steps, damping_ref, phases_ref, packed_ref, own_ref, other_ref,
    out_ref, square_ref
):
    lanes = 4 * bands
    groups = bands // 4
    chunks, (above_log, above_phase) = unpack_sum(own_ref, other_ref, bands)
    at = lax.broadcasted_iota(jnp.int32, (steps, bands), 0)
    rates = jnp.log(damping_ref[...])
    phases = phases_ref[...]
    summed_log = jnp.broadcast_to(above_log, (steps, bands))
    summed_phase = jnp.broadcast_to(above_phase, (steps, bands))
    for step in range(steps):
        summed_log = summed_log + jnp.where(at <= step, rates[step : step + 1], 0.0)
        summed_phase = summed_phase + jnp.where(at <= step, phases[step : step + 1], 0.0)
    magnitude = jnp.exp(summed_log)
    both = jnp.concatenate(
        [magnitude * jnp.cos(summed_phase), -magnitude * jnp.sin(summed_phase)], axis=1
    )
    wide = lax.broadcasted_iota(jnp.int32, (steps, steps * bands), 1) // bands
    place = lax.broadcasted_iota(jnp.int32, (steps, steps * bands), 0)
    spreading = jnp.where(wide == place, 1.0, 0.0).astype(BF16)
    factor = jnp.zeros((2 * bands, steps * bands), F32)
    for _ in range(3):
        piece = both.astype(BF16)
        both = both - piece.astype(F32)
        factor = factor + lax.dot_general(
            piece, spreading, (((0,), (0,)), ((), ())), preferred_element_type=F32
        )
    row = packed_ref[...] + jnp.concatenate(chunks, axis=1)
    row_real, row_imag = (row[:bands], row[bands:])
    factor_real, factor_imag = (factor[:bands], factor[bands:])
    stepped = (
        factor_real * row_real - factor_imag * row_imag,
        factor_real * row_imag + factor_imag * row_real,
    )
    squares = jnp.sum(stepped[0] * stepped[0] + stepped[1] * stepped[1], keepdims=True)
    square_ref[...] = jnp.broadcast_to(squares, square_ref.shape)
    out_ref[:bands, :] = stepped[0]
    out_ref[bands:, :] = stepped[1]


def relayout_kernel(bands, steps, stepped_ref, out_ref, work, mixed):
    lanes = 4 * bands
    groups = bands // 4
    for part in range(2):
        for chunk in range(steps // 4):
            work[part, chunk, :bands] = stepped_ref[
                part * bands : (part + 1) * bands, chunk * lanes : (chunk + 1) * lanes
            ]
    for part in range(2):
        for chunk in range(steps // 4):
            blocks = [work[part, chunk, pl.ds(k, groups, stride=4), :] for k in range(4)]
            for k, block in enumerate(swap_blocks(blocks)):
                first = (chunk * 4 + k) * groups * 2 + part
                mixed[pl.ds(first, groups, stride=2), :] = block
    out_ref[...] = mixed[: out_ref.shape[0], :]


def call(kernel, shapes, scratch, flops, moved, spaces, *operands):
    return pl.pallas_call(
        kernel,
        out_shape=shapes,
        in_specs=[pl.BlockSpec(memory_space=space) for space in spaces],
        out_specs=[pl.BlockSpec(memory_space=pltpu.VMEM)] * len(shapes),
        scratch_shapes=scratch,
        compiler_params=pltpu.CompilerParams(vmem_limit_bytes=VMEM_LIMIT),
        cost_estimate=pl.CostEstimate(flops=flops, bytes_accessed=moved, transcendentals=0),
    )(*operands)


def shards(
    row_less, row_great, coupling, damping, phases, lesser_hist, advanced_hist, retarded_hist
):
    bands = coupling.shape[0]
    lanes = 4 * bands
    groups = bands // 4
    steps = row_less.shape[1]
    rows = lesser_hist.shape[1]
    hist_count, row_count = (lax.axis_size("hist"), lax.axis_size("row"))
    ratio = hist_count // row_count
    all_steps = steps * hist_count
    weight = float(all_steps * bands) ** (-0.5)
    taken = steps * bands
    sds = jax.ShapeDtypeStruct

    def grouped(x):
        x = x.reshape(2, steps, groups, lanes).transpose(1, 2, 0, 3)
        return x.reshape(steps * groups * 2, lanes)

    retarded = retarded_hist.transpose(0, 2, 1, 3)
    vmem = pltpu.VMEM
    (order,) = call(
        functools.partial(order_kernel, bands, steps, ratio),
        [sds((ratio * taken, bands * WINDOW), BF16)],
        [],
        10**10,
        10**7,
        [],
    )
    send, packed = call(
        functools.partial(energy_kernel, bands, steps),
        [sds((taken + EXTRA, lanes), BF16), sds((2 * bands, taken), F32)],
        [
            vmem((2, steps * groups * 2 + 8, lanes), F32),
            vmem((2, 2, steps // 4 * bands + 8, lanes), F32),
        ],
        10**8,
        10**6,
        [pl.ANY] + [vmem] * 5,
        order,
        grouped(row_less),
        grouped(row_great),
        coupling,
        damping,
        phases,
    )
    arrived = [swap_places(send, turn) for turn in range(ratio)]
    column, give = call(
        functools.partial(column_kernel, bands, steps, rows, weight),
        [sds((groups * rows, lanes), F32), sds((groups * rows + 2 * EXTRA, lanes), BF16)],
        [],
        10**9,
        4 * 10**6,
        [vmem] * 2,
        retarded,
        send,
    )

    def add(own, other, kind):
        (out,) = call(
            add_kernel, [sds(own.shape, kind)], [], 10**10, 10**6, [vmem] * 2, own, other
        )
        return out

    got = crossed(give, "hist", 1)
    summed = sds((steps // 4 * 2 * bands + EXTRA, lanes), BF16)
    histories = [lesser_hist.transpose(0, 2, 1, 3), advanced_hist.transpose(0, 2, 1, 3)]
    (rights,) = call(
        functools.partial(right_kernel, bands, steps, rows, ratio, 0),
        [sds((steps * 2 * bands // 4 * WINDOW, 2 * lanes), BF16)],
        [],
        10**4,
        10**4,
        [vmem] * 2,
        *histories,
    )
    order_first, rights = lax.optimization_barrier((order, rights))
    partial_row = []
    for turn in reversed(range(ratio)):
        operands = [order_first] + histories if turn else [order, rights, rights]
        operands += [arrived[turn], *partial_row]
        partial_row = call(
            functools.partial(row_kernel, bands, steps, rows, weight, ratio, turn),
            [summed if turn == 0 else sds((2 * bands + 8, taken), F32)],
            [],
            10**4,
            10**4,
            [vmem] * len(operands),
            *operands,
        )
    partial_row = partial_row[0]
    bit = 1
    while 2 * bit < row_count:
        (partial_row,) = call(
            functools.partial(narrow_kernel, bands),
            [summed],
            [],
            10**4,
            10**4,
            [vmem] * 2,
            partial_row,
            crossed(partial_row, "row", bit),
        )
        bit *= 2
    other = crossed(partial_row, "row", bit)
    column = add(column, got, BF16)
    got = crossed(column, "hist", hist_count // 2)
    stepped, squares = call(
        functools.partial(step_kernel, bands, steps),
        [sds((2 * bands, taken), F32), sds((8, lanes), F32)],
        [],
        10**10,
        10**6,
        [vmem] * 5,
        damping,
        phases,
        packed,
        partial_row,
        other,
    )
    (stepped,) = call(
        functools.partial(relayout_kernel, bands, steps),
        [sds((steps * groups * 2, lanes), F32)],
        [vmem((2, steps // 4, bands + 8, lanes), F32), vmem((steps * groups * 2 + 8, lanes), F32)],
        10**10,
        10**6,
        [vmem],
        stepped,
    )
    ahead = [hist_count >> k for k in range(1, hist_count.bit_length() - 1)]
    beside = ahead[1:] + [1, None]
    for bit, each in zip([1] + ahead, beside):
        other = crossed(squares, "hist", bit)
        if each:
            column = add(column, got, F32)
            got = crossed(column, "hist", each)
            squares = add(squares, other, F32)
    got, other = lax.optimization_barrier((got, other))
    stepped, column = call(
        functools.partial(final_kernel, float(2 * all_steps * bands * bands)),
        [sds(stepped.shape, F32), sds((2, rows, bands * bands), F32)],
        [],
        10**6,
        10**6,
        [vmem] * 5,
        stepped,
        squares,
        other,
        column,
        got,
    )
    stepped = stepped.reshape(steps, groups, 2, lanes).transpose(2, 0, 1, 3)
    return (stepped.reshape(2, steps, bands * bands), column)


def solution(mesh):
    return jax.shard_map(
        shards,
        mesh=mesh,
        in_specs=(
            P(None, "hist", None),
            P(None, "hist", None),
            P(),
            P("hist", None),
            P("hist", None),
            P(None, "row", "hist", None),
            P(None, "row", "hist", None),
            P(None, "row", "hist", None),
        ),
        out_specs=(P(None, "hist", None), P(None, "row", None)),
        check_vma=False,
    )
```
